32 devices in a mesh: tile: 8 (over z, x), depth: 4 (over y, core).
Axes of the slice: x: 2, y: 2, z: 4, core: 2. Of those that a mesh axis runs over, the one named last changes fastest.
Arguments:
- substrate_start: float32 [4, 2, 16, 16, 1024], P(None, None, 'depth', 'tile'), may hold values from -6 to 6
- adatom_start: float32 [40, 2, 24576], P(None, None, ('tile', 'depth')), may hold values from -6 to 6
- disorder: float32 [16, 16, 1024], P('depth', 'tile'), may hold values from -0.4 to 0.4
- adatom_block: float32 [40, 40], replicated, as said below
- coupling: float32 [4, 40], replicated, may hold values from -1 to 1
- adatom_tile: int32 [24576, 1], P(('tile', 'depth')), may hold values from 0 to 7; in each aligned block of 768 rows (0 to 767, 768 to 1535, ...) at most 192 rows name the same one
- adatom_spot: int32 [24576], P(('tile', 'depth')), may hold values from 0 to 2047
Outputs:
- substrate_prev: float32 [4, 2, 16, 16, 1024], P(None, None, 'depth', 'tile')
- substrate_last: float32 [4, 2, 16, 16, 1024], P(None, None, 'depth', 'tile')
- adatom_prev: float32 [40, 2, 24576], P(None, None, ('tile', 'depth'))
- adatom_last: float32 [40, 2, 24576], P(None, None, ('tile', 'depth'))
The draws below stay inside these ranges and needn't reach their ends.
Inputs may be any that keep to these rules, and one draw needn't show every extreme that they name: `adatom_tile`: among the adatoms of one device, no tile is named by more than 192. adatom_block is symmetric.
All inputs are finite; a program needn't handle non-finite values.
Results may differ from the reference program's by a relative error of at most 0.0003.
Values sent between devices are 32-bit elements; how exact they have to be, the bound alone decides.
A program may use at most 64 MiB of HBM per device.

```python
import math
import jax
import jax.numpy as jnp
import numpy as np
from jax import lax

ORB = 4
VECS = 2
CX = 2
NY = 1024
ORBA = 40
ADEV = 768
STEPS = 3
NL = 16
NX = 16
NAD = 24576
CAP = 192
N_TILE = 8


def draw_adatom_block(key, part):
    key = jax.random.fold_in(key, 7)
    raw = jax.random.normal(key, (ORBA, ORBA), jnp.float32)
    return ((raw + raw.T) * (0.5 / math.sqrt(ORBA))).astype(jnp.float32)


def with_ends(values, rng, low, top_value):
    extent = values.shape
    place = [jax.random.randint(jax.random.fold_in(rng, axis), (), 0, extent[axis]) for axis in range(len(extent))]
    values = values.at[tuple(place)].set(low)
    longest = extent.index(max(extent))
    place[longest] = (place[longest] + 1) % extent[longest]
    return values.at[tuple(place)].set(top_value)


def shard_levels(own_key, extent, shards, smallest, largest):
    def one(position, shards_of):
        draws = jax.random.uniform(jax.random.fold_in(jax.random.fold_in(own_key, 6), position), (shards_of,), jnp.float32, smallest / len(shards), largest / len(shards))
        return jnp.repeat(jnp.exp(draws), extent[position] // shards_of).reshape((-1,) + (1,) * (len(extent) - position - 1))

    gain = one(*shards[0])
    for cut in shards[1:]:
        gain = gain * one(*cut)
    return gain


def routed_block(rng, own, number, rows, amount, top, most, slope):
    order = jax.random.permutation(rng, amount)
    heavy_load, ordinary = load_shares(amount, rows * top, most, slope, True), load_shares(amount, rows * top, most, slope, False)
    places = jnp.arange(amount)

    def named(lengths, rotation):
        used = int((lengths > 0).sum())
        fixed = max(1, used // 4)
        shifted = fixed + (places - fixed + rotation * (used - fixed)) % max(1, amount - fixed)
        return jnp.zeros((amount,), jnp.int32).at[order[jnp.where(places < fixed, places, shifted)]].set(jnp.asarray(lengths, jnp.int32))

    lengths = jnp.where(number % 4 == 0, named(heavy_load, number // 4), named(ordinary, number - number // 4 - 1))
    mixed = jax.random.permutation(jax.random.fold_in(own, 3), amount)
    giver, receiver = mixed[0:amount // 2 * 2:2], mixed[1:amount // 2 * 2:2]
    room = jnp.minimum(lengths[giver] - 1, most - lengths[receiver]) // 2
    room = jnp.where((giver == order[0]) | (receiver == order[0]) | (lengths[receiver] == 0), 0, jnp.maximum(room, 0))
    shifted = jax.random.randint(jax.random.fold_in(own, 4), (amount // 2,), 0, 1 << 20) % (room + 1)
    lengths = lengths.at[giver].add(-shifted).at[receiver].add(shifted)
    labels = jnp.searchsorted(jnp.cumsum(lengths), jnp.arange(rows * top), side="right").astype(jnp.int32)
    grid = labels.reshape(top, rows).T
    grid = grid[jax.random.permutation(jax.random.fold_in(own, 1), rows)]
    rotation = jax.random.randint(jax.random.fold_in(own, 2), (rows, 1), 0, top)
    return jnp.take_along_axis(grid, (jnp.arange(top)[None, :] + rotation) % top, axis=1)


def load_shares(number_of, total, limit, slope, full):
    loads = [(1 << 20) // math.isqrt(grade ** slope) + 1 for grade in range(1, number_of + 1)]
    largest = limit if full else min(limit, max(-(-total // number_of), total * loads[0] // sum(loads)))
    least = 1 if total - largest >= number_of - 1 else 0
    given, spare = [largest] + [least] * (number_of - 1), total - largest - least * (number_of - 1)
    while spare > 0:
        candidates = [i for i in range(1, number_of) if given[i] < largest] or [i for i in range(1, number_of) if given[i] < limit]
        pool, budget = sum([loads[i] for i in candidates]), spare
        for i in candidates:
            addition = min(limit - given[i], max(1, budget * loads[i] // pool), spare)
            given[i] = given[i] + addition
            spare = spare - addition
    return np.array(given)


def normal_values(own_key, extent, deviation, bound, cuts=(), kind=jnp.bfloat16):
    entries = jax.random.normal(own_key, extent, jnp.float32) * deviation
    if len(cuts) > 0:
        entries = shard_levels(own_key, extent, cuts, -0.22, 0.18) * entries
    return jnp.clip(entries, min=-bound, max=bound).astype(kind)


def setup_inputs(seed: int = 0) -> dict:
    splits = jax.random.split(jax.random.key(seed), 8)
    substrate_start = normal_values(splits[0], (ORB, VECS, NL, NX, NY), 1.0, 6.0, ((2, 4), (3, 8)), jnp.float32)
    adatom_start = normal_values(splits[1], (ORBA, VECS, NAD), 1.0, 6.0, ((2, 32),), jnp.float32)
    disorder = jnp.clip(jax.random.uniform(splits[2], (NL, NX, NY), jnp.float32, -0.4, 0.4) * shard_levels(splits[2], (NL, NX, NY), ((0, 4), (1, 8)), -0.4, 0.0), -0.4, 0.4)
    adatom_block = draw_adatom_block(jax.random.fold_in(splits[7], 71), 0)
    coupling = normal_values(splits[4], (ORB, ORBA), ORBA ** -0.5, 1.0, (), jnp.float32)
    adatom_tile_keys = jax.random.split(jax.random.fold_in(splits[5], 1), NAD // ADEV)
    adatom_tile_turns = jax.random.permutation(jax.random.fold_in(splits[5], 3), NAD // ADEV)
    adatom_tile = jax.vmap(lambda own, number: routed_block(jax.random.fold_in(splits[5], 2), own, number, ADEV, N_TILE, 1, CAP, 2))(adatom_tile_keys, adatom_tile_turns).reshape((NAD, 1))
    adatom_spot = with_ends(jax.random.randint(splits[6], (NAD,), 0, CX * NY), jax.random.fold_in(splits[6], 1), 0, (CX * NY) - 1).astype(jnp.int32)
    return {"substrate_start": substrate_start, "adatom_start": adatom_start, "disorder": disorder, "adatom_block": adatom_block, "coupling": coupling, "adatom_tile": adatom_tile, "adatom_spot": adatom_spot}


hopping = 0.12
chemical = 0.15
pairing = 0.3


def substrate_terms(padded, field, disorder):
    beside = padded[:, :, 2:, 1:-1] + padded[:, :, :-2, 1:-1]
    beside = beside + padded[:, :, 1:-1, 2:] + padded[:, :, 1:-1, :-2]
    widened = jnp.pad(field, ((0, 0), (0, 0), (0, 0), (0, 0), (1, 1)))
    beside = beside + widened[..., 2:] + widened[..., :-2]
    signs = jnp.array([1.0, 1.0, -1.0, -1.0], jnp.float32).reshape(4, 1, 1, 1, 1)
    onsite = (disorder - chemical)[None, None] * field - hopping * beside
    partner = jnp.concatenate([field[2:], field[:2]], axis=0)
    return signs * onsite + pairing * partner


def operate(sub, adatoms, disorder, adatom_block, coupling, site):
    padded = jnp.pad(sub, ((0, 0), (0, 0), (1, 1), (1, 1), (0, 0)))
    sub_out = substrate_terms(padded, sub, disorder)
    orbs, vecs, layers, rows, cols = sub.shape
    surface = sub[:, :, 0].reshape(orbs * vecs, rows * cols)
    below = surface[:, site].reshape(orbs, vecs, -1)
    ad_out = jnp.einsum("ab,bvn->avn", adatom_block, adatoms, precision=lax.Precision.HIGHEST)
    ad_out = ad_out + jnp.einsum("oa,ovn->avn", coupling, below, precision=lax.Precision.HIGHEST)
    contrib = jnp.einsum("oa,avn->ovn", coupling, adatoms, precision=lax.Precision.HIGHEST)
    contrib = contrib.reshape(orbs * vecs, -1)
    added = jnp.zeros((orbs * vecs, rows * cols), jnp.float32).at[:, site].add(contrib)
    sub_out = sub_out.at[:, :, 0].add(added.reshape(orbs, vecs, rows, cols))
    return sub_out, ad_out


def reference(substrate_start, adatom_start, disorder, adatom_block, coupling, adatom_tile, adatom_spot):
    site = (adatom_tile[:, 0] * (CX * NY) + adatom_spot).astype(jnp.int32)
    prev_sub, prev_ad = substrate_start, adatom_start
    cur_sub, cur_ad = operate(prev_sub, prev_ad, disorder, adatom_block, coupling, site)
    for step in range(STEPS - 1):
        new_sub, new_ad = operate(cur_sub, cur_ad, disorder, adatom_block, coupling, site)
        new_sub = 2.0 * new_sub - prev_sub
        new_ad = 2.0 * new_ad - prev_ad
        prev_sub, prev_ad = cur_sub, cur_ad
        cur_sub, cur_ad = new_sub, new_ad
    return prev_sub, cur_sub, prev_ad, cur_ad
```

```python
import functools

import jax
import jax.numpy as jnp
from jax import lax
from jax.experimental import pallas as pl
from jax.experimental.pallas import tpu as pltpu
from jax.sharding import PartitionSpec as P

STEPS = 3
HOPPING = 0.12
CHEMICAL = 0.15
PAIRING = 0.3
ORB = 4
GROUP = 8
LIVE, HIGH, LOW = 12, 13, 14

MESH = pl.DeviceIdType.MESH
HIGHEST = lax.Precision.HIGHEST
NN = (((1,), (0,)), ((), ()))
NT = (((1,), (1,)), ((), ()))


def each(count, body):
    if count <= GROUP:
        for i in range(count):
            body(i)
    else:

        def run(i, carry):
            body(i)
            return carry

        lax.fori_loop(0, count, run, 0)


def exact(a, b, dims=NN):
    return lax.dot_general(a, b, dims, precision=HIGHEST, preferred_element_type=jnp.float32)


def product(a, b, dims=NN):
    return lax.dot_general(a, b, dims, preferred_element_type=jnp.float32)


def halves(x):
    first = x.astype(jnp.bfloat16).astype(jnp.float32)
    return first, (x - first).astype(jnp.bfloat16).astype(jnp.float32)


def iota(shape, dim):
    return lax.broadcasted_iota(jnp.int32, shape, dim)


def kernel(
    tiles, depths,
    s0, adatoms, disorder, block, coupling, tile_of, spot_of,
    s2, s3, a2, a3,
    s1, hx, hl, top, send, got, lhs, low_t, high, scat, red_a, red_b, ans, back, proj, rank_t, a1,
    hx_s, hx_r, hl_s, hl_r, top_s, top_r, go_s, go_r, ra_s, ra_r, rb_s, rb_r, an_s, an_r,
):
    t = lax.axis_index("tile")
    d = lax.axis_index("depth")
    rows, layers, fields = s0.shape[:3]
    count = tile_of.shape[1]
    slots = send.shape[2]
    lines = rows * 8
    states = [s0, s1, s2, s3]

    barrier = pltpu.get_barrier_semaphore()

    def greet_tile(i):
        pl.semaphore_signal(
            barrier, inc=1, device_id=(lax.rem(t + i + 1, tiles), d), device_id_type=MESH
        )

    def greet_depth(i):
        pl.semaphore_signal(
            barrier, inc=1, device_id=(t, lax.rem(d + i + 1, depths)), device_id_type=MESH
        )

    each(tiles - 1, greet_tile)
    each(depths - 1, greet_depth)

    for side, (edge_t, edge_d) in enumerate(((0, 0), (tiles - 1, depths - 1))):

        @pl.when(t == edge_t)
        def _():
            hx[:, side] = jnp.zeros_like(hx[:, side])

        @pl.when(d == edge_d)
        def _():
            hl[:, side] = jnp.zeros_like(hl[:, side])

    pl.semaphore_wait(barrier, tiles - 1 + depths - 1)

    def halo(k, side):
        state = states[k]
        step = 1 if side == 0 else -1
        row = rows - 1 if side == 0 else 0
        layer = layers - 1 if side == 0 else 0
        along_x = pltpu.make_async_remote_copy(
            src_ref=state.at[row], dst_ref=hx.at[k, side],
            send_sem=hx_s.at[k, side], recv_sem=hx_r.at[k, side],
            device_id=(lax.rem(t + step + tiles, tiles), d), device_id_type=MESH,
        )
        along_l = pltpu.make_async_remote_copy(
            src_ref=state.at[:, layer], dst_ref=hl.at[k, side],
            send_sem=hl_s.at[k, side], recv_sem=hl_r.at[k, side],
            device_id=(t, lax.rem(d + step + depths, depths)), device_id_type=MESH,
        )
        return along_x, along_l

    def sends(side):
        if side == 0:
            return t < tiles - 1, d < depths - 1
        return t > 0, d > 0

    def takes(side):
        if side == 0:
            return t > 0, d > 0
        return t < tiles - 1, d < depths - 1

    def halo_start(k):
        for side in range(2):
            for copy, there in zip(halo(k, side), sends(side)):
                pl.when(there)(copy.start)

    def halo_wait(k):
        for side in range(2):
            for copy, there in zip(halo(k, side), takes(side)):
                pl.when(there)(copy.wait_recv)

    def halo_sent(k):
        for side in range(2):
            for copy, there in zip(halo(k, side), sends(side)):
                pl.when(there)(copy.wait_send)

    def top_copy(k, i):
        return pltpu.make_async_remote_copy(
            src_ref=top.at[k], dst_ref=top.at[k],
            send_sem=top_s.at[k, i], recv_sem=top_r.at[k],
            device_id=(t, i + 1), device_id_type=MESH,
        )

    def top_start(k):
        @pl.when(d == 0)
        def _():
            top[k] = states[k][:, 0]
            each(depths - 1, lambda i: top_copy(k, i).start())

    def top_wait(k):
        pl.when(d > 0)(lambda: top_copy(k, 0).wait_recv())

    def peer(i):
        return lax.rem(t + i + 1, tiles)

    def go_copy(other, to):
        return pltpu.make_async_remote_copy(
            src_ref=send.at[other], dst_ref=got.at[to],
            send_sem=go_s.at[other], recv_sem=go_r.at[to],
            device_id=(other, d), device_id_type=MESH,
        )

    def answer_copy(k, other, to):
        return pltpu.make_async_remote_copy(
            src_ref=ans.at[k, other], dst_ref=back.at[k, to],
            send_sem=an_s.at[k, other], recv_sem=an_r.at[k, to],
            device_id=(other, d), device_id_type=MESH,
        )

    def partial_copy(part, i):
        if part == 0:
            src, dst, ss, rs = scat.at[pl.ds(0, 8)], red_a, ra_s, ra_r
        else:
            src, dst, ss, rs = scat.at[pl.ds(8, 17)], red_b, rb_s, rb_r
        return pltpu.make_async_remote_copy(
            src_ref=src, dst_ref=dst.at[i], send_sem=ss, recv_sem=rs.at[i],
            device_id=(t, 0), device_id_type=MESH,
        )

    def reduce_wait(part):
        first, length = ((0, 8), (8, 17))[part]
        buffer = (red_a, red_b)[part]

        def add(i):
            partial_copy(part, i).wait_recv()
            scat[pl.ds(first, length)] += buffer[i]

        each(depths - 1, add)

    lane = iota((8, 8, 128), 2)
    sub = iota((8, 8, 128), 1)
    plus = iota((8, 8, 128), 0) % ORB < 2

    def stencil(k):
        field, out = states[k], states[k + 1]
        for x in range(rows):
            for l in range(layers):
                f = field[x, l]
                beside = field[x, l - 1] if l > 0 else hl[k, 0, x]
                beside += field[x, l + 1] if l < layers - 1 else hl[k, 1, x]
                beside += field[x - 1, l] if x > 0 else hx[k, 0, l]
                beside += field[x + 1, l] if x < rows - 1 else hx[k, 1, l]
                r = pltpu.roll(f, 1, 2)
                c = jnp.where(sub == 0, 0.0, pltpu.roll(r, 1, 1))
                beside += jnp.where(lane == 0, c, r)
                r = pltpu.roll(f, 127, 2)
                c = jnp.where(sub == 7, 0.0, pltpu.roll(r, 7, 1))
                beside += jnp.where(lane == 127, c, r)
                onsite = (disorder[x, l] - CHEMICAL)[None] * f - HOPPING * beside
                partner = jnp.concatenate([f[2:4], f[0:2], f[6:8], f[4:6]], axis=0)
                new = jnp.where(plus, onsite, -onsite) + PAIRING * partner
                if k > 0:
                    new = 2.0 * new - states[k - 1][x, l]
                out[x, l] = new

    halo_start(0)
    top_start(0)

    b, c = block[...], coupling[...]
    cb = exact(c, b)
    proj[0:4] = c
    proj[4:8] = cb
    proj[8:12] = exact(cb, b)
    proj[12:16] = jnp.zeros((4, b.shape[0]), jnp.float32)
    pair1 = exact(c, c, NT)
    pair2 = exact(cb, c, NT)
    values = exact(proj[...], adatoms[...])
    values = jnp.concatenate([values[:, :count], values[:, count:]], axis=0)
    spot = spot_of[...]
    row = iota(values.shape, 0)
    values = jnp.where(row == LIVE, 1.0, values)
    values = jnp.where(row == HIGH, (spot // 128).astype(jnp.float32), values)
    values = jnp.where(row == LOW, (spot % 128).astype(jnp.float32), values)
    owner = (iota((tiles, count), 0) == tile_of[...]).astype(jnp.float32)
    earlier = (iota((count, count), 0) < iota((count, count), 1)).astype(jnp.float32)
    before = product(owner.astype(jnp.bfloat16), earlier.astype(jnp.bfloat16))
    rank = jnp.sum(owner * before, axis=0, keepdims=True).astype(jnp.int32)
    rank_t[...] = (iota((slots, count), 0) == rank).astype(jnp.float32).astype(jnp.bfloat16)
    parts = jnp.concatenate(halves(values), axis=0)

    def compact(g):
        chosen = [
            jnp.where(tile_of[...] == g * GROUP + i, parts, 0.0).astype(jnp.bfloat16)
            for i in range(GROUP)
        ]
        packed = product(jnp.concatenate(chosen, axis=0), rank_t[...], NT)
        for i in range(GROUP):
            at = i * 64
            send[g * GROUP + i] = packed[at : at + 32] + packed[at + 32 : at + 64]

    each(tiles // GROUP, compact)
    each(tiles - 1, lambda i: go_copy(peer(i), t).start())
    got[t] = send[t]

    halo_wait(0)
    stencil(0)

    each(tiles - 1, lambda i: go_copy(peer(i), peer(i)).wait_recv())

    order = [v * 16 + j * 4 + o for j in range(STEPS) for v in range(2) for o in range(ORB)]
    order.append(LIVE)
    terms = len(order)

    def scatter(g):
        for i in range(GROUP):
            u = g * GROUP + i
            data = got[u]
            first, second = halves(data)
            here = iota((lines, slots), 0).astype(jnp.float32) == data[HIGH : HIGH + 1]
            high[u] = here.astype(jnp.float32)
            low = iota((128, slots), 0).astype(jnp.float32) == data[LOW : LOW + 1]
            low_t[u] = low.astype(jnp.float32).astype(jnp.bfloat16)
            for at, q in enumerate(order):
                for p, part in enumerate((first, second)):
                    if q == LIVE and p == 1:
                        continue
                    line = (p * terms + at) * lines
                    lhs[line : line + lines, i * slots : (i + 1) * slots] = jnp.where(
                        here, part[q : q + 1], 0.0
                    ).astype(jnp.bfloat16)
        total = jnp.zeros((lhs.shape[0], 128), jnp.float32)
        for i in range(GROUP):
            total += product(
                lhs[:, i * slots : (i + 1) * slots], low_t[g * GROUP + i], NT
            )
        half = terms * lines
        merged = total[: half - lines] + total[half:]
        merged = merged.reshape(terms - 1, rows, 8, 128)
        counted = total[half - lines : half].reshape(rows, 8, 128)
        if tiles == GROUP:
            scat[0 : terms - 1] = merged
            scat[terms - 1] = counted
        else:
            scat[0 : terms - 1] += merged
            scat[terms - 1] += counted

    if tiles > GROUP:
        scat[...] = jnp.zeros_like(scat)
    each(tiles // GROUP, scatter)

    @pl.when(d > 0)
    def _():
        partial_copy(0, d - 1).start()
        partial_copy(1, d - 1).start()

    @pl.when(d == 0)
    def _():
        reduce_wait(0)
        for x in range(rows):
            s1[x, 0] += scat[0:8, x]

    halo_start(1)
    top_start(1)

    def gather(k):
        top_wait(k)
        first, second = halves(top[k].reshape(rows * 8 * 8, 128))
        both = jnp.concatenate([first, second], axis=0).astype(jnp.bfloat16)

        def one(u):
            found = product(both, low_t[u])
            half = rows * 64
            found = (found[:half] + found[half:]).reshape(rows, 8, 8, slots)
            found = found * high[u].reshape(rows, 1, 8, slots)
            ans[k, u] = jnp.sum(jnp.sum(found, axis=0), axis=1)

        each(tiles, one)
        each(tiles - 1, lambda i: answer_copy(k, peer(i), t).start())
        back[k, t] = ans[k, t]

    def below(k):
        each(tiles - 1, lambda i: answer_copy(k, peer(i), peer(i)).wait_recv())
        first, second = halves(back[k].reshape(tiles * 8, slots))
        both = jnp.concatenate([first, second], axis=0).astype(jnp.bfloat16)
        found = product(both, rank_t[...])
        found = (found[: tiles * 8] + found[tiles * 8 :]).reshape(tiles, 8, count)
        found = jnp.sum(found * owner.reshape(tiles, 1, count), axis=0)
        return jnp.concatenate([found[0:4], found[4:8]], axis=1)

    ct = exact((iota(b.shape, 0) == iota(b.shape, 1)).astype(jnp.float32), c, NT)

    def adatom_part(k, vector):
        return exact(b, vector) + exact(ct, below(k))

    def mixed(pair, state, x):
        sums = []
        for v in range(2):
            for o in range(ORB):
                total = None
                for m in range(ORB):
                    term = pair[o : o + 1, m : m + 1] * state[x, 0, v * ORB + m]
                    total = term if total is None else total + term
                sums.append(total[None])
        return jnp.concatenate(sums, axis=0)

    gather(0)
    halo_wait(1)
    stencil(1)

    @pl.when(d == 0)
    def _():
        reduce_wait(1)
        for x in range(rows):
            extra = scat[8:16, x] + scat[24, x][None] * mixed(pair1, s0, x)
            s2[x, 0] += 2.0 * extra

    halo_start(2)
    top_start(2)
    gather(1)
    a1[...] = adatom_part(0, adatoms[...])
    gather(2)
    halo_wait(2)
    stencil(2)

    @pl.when(d == 0)
    def _():
        for x in range(rows):
            pairs = mixed(pair2, s0, x) + mixed(pair1, s1, x)
            extra = scat[16:24, x] + scat[24, x][None] * pairs
            s3[x, 0] += 2.0 * (2.0 * extra - scat[0:8, x])

    a2[...] = 2.0 * adatom_part(1, a1[...]) - adatoms[...]
    a3[...] = 2.0 * adatom_part(2, a2[...]) - a1[...]

    each(tiles - 1, lambda i: go_copy(peer(i), t).wait_send())
    for k in range(STEPS):
        halo_sent(k)
        each(tiles - 1, lambda i: answer_copy(k, peer(i), t).wait_send())

    @pl.when(d == 0)
    def _():
        for k in range(STEPS):
            each(depths - 1, lambda i: top_copy(k, i).wait_send())

    @pl.when(d > 0)
    def _():
        partial_copy(0, d - 1).wait_send()
        partial_copy(1, d - 1).wait_send()


def per_device(
    substrate_start, adatom_start, disorder, adatom_block, coupling, adatom_tile, adatom_spot
):
    tiles, depths = lax.axis_size("tile"), lax.axis_size("depth")
    count = adatom_spot.shape[0]
    orbs, vecs, layers, rows, cols = substrate_start.shape
    orba = adatom_block.shape[0]
    capacity = 2 * count // tiles
    slots = -(-capacity // 128) * 128
    sites = substrate_start.reshape(orbs, vecs, layers, rows, 8, 128)
    sites = sites.transpose(3, 2, 1, 0, 4, 5).reshape(rows, layers, 8, 8, 128)
    potential = disorder.reshape(layers, rows, 8, 128).transpose(1, 0, 2, 3)
    vectors = adatom_start.reshape(orba, vecs * count)
    f32 = jnp.float32
    state = jax.ShapeDtypeStruct(sites.shape, f32)
    flat = jax.ShapeDtypeStruct(vectors.shape, f32)
    lines = rows * 8
    dma = pltpu.SemaphoreType.DMA
    vmem = pl.BlockSpec(memory_space=pltpu.VMEM)
    s2, s3, a2, a3 = pl.pallas_call(
        functools.partial(kernel, tiles, depths),
        out_shape=(state, state, flat, flat),
        in_specs=[vmem] * 7,
        out_specs=(vmem,) * 4,
        scratch_shapes=[
            pltpu.VMEM(sites.shape, f32),
            pltpu.VMEM((STEPS, 2, layers, 8, 8, 128), f32),
            pltpu.VMEM((STEPS, 2, rows, 8, 8, 128), f32),
            pltpu.VMEM((STEPS, rows, 8, 8, 128), f32),
            pltpu.VMEM((tiles, 32, slots), f32),
            pltpu.VMEM((tiles, 32, slots), f32),
            pltpu.VMEM((49 * lines, GROUP * slots), jnp.bfloat16),
            pltpu.VMEM((tiles, 128, slots), jnp.bfloat16),
            pltpu.VMEM((tiles, lines, slots), f32),
            pltpu.VMEM((25, rows, 8, 128), f32),
            pltpu.VMEM((depths - 1, 8, rows, 8, 128), f32),
            pltpu.VMEM((depths - 1, 17, rows, 8, 128), f32),
            pltpu.VMEM((STEPS, tiles, 8, slots), f32),
            pltpu.VMEM((STEPS, tiles, 8, slots), f32),
            pltpu.VMEM((16, orba), f32),
            pltpu.VMEM((slots, count), jnp.bfloat16),
            pltpu.VMEM(vectors.shape, f32),
            dma((STEPS, 2)), dma((STEPS, 2)), dma((STEPS, 2)), dma((STEPS, 2)),
            dma((STEPS, depths - 1)), dma((STEPS,)),
            dma((tiles,)), dma((tiles,)),
            dma, dma((depths - 1,)), dma, dma((depths - 1,)),
            dma((STEPS, tiles)), dma((STEPS, tiles)),
        ],
        compiler_params=pltpu.CompilerParams(
            collective_id=0, has_side_effects=True, vmem_limit_bytes=56 * 1024 * 1024
        ),
    )(
        sites, vectors, potential, adatom_block, coupling,
        adatom_tile.reshape(1, count), adatom_spot.reshape(1, count),
    )

    def unpack(s):
        s = s.reshape(rows, layers, vecs, orbs, 8, 128).transpose(3, 2, 1, 0, 4, 5)
        return s.reshape(substrate_start.shape)

    return unpack(s2), unpack(s3), a2.reshape(adatom_start.shape), a3.reshape(adatom_start.shape)


def solution(mesh):
    in_specs = (
        P(None, None, "depth", "tile", None),
        P(None, None, ("tile", "depth")),
        P("depth", "tile", None),
        P(),
        P(),
        P(("tile", "depth"), None),
        P(("tile", "depth")),
    )
    out_specs = (
        P(None, None, "depth", "tile", None),
        P(None, None, "depth", "tile", None),
        P(None, None, ("tile", "depth")),
        P(None, None, ("tile", "depth")),
    )
    return jax.shard_map(
        per_device, mesh=mesh, in_specs=in_specs, out_specs=out_specs, check_vma=False
    )
```

```python
import functools

import jax
import jax.numpy as jnp
from jax import lax
from jax.experimental import pallas as pl
from jax.experimental.pallas import tpu as pltpu
from jax.sharding import PartitionSpec as P

STEPS = 3
HOPPING = 0.12
CHEMICAL = 0.15
PAIRING = 0.3
ORB = 4
GROUP = 8
LIVE, HIGH, LOW = 12, 13, 14

MESH = pl.DeviceIdType.MESH
HIGHEST = lax.Precision.HIGHEST
NN = (((1,), (0,)), ((), ()))
NT = (((1,), (1,)), ((), ()))


def each(count, body):
    if count <= GROUP:
        for i in range(count):
            body(i)
    else:

        def run(i, carry):
            body(i)
            return carry

        lax.fori_loop(0, count, run, 0)


def exact(a, b, dims=NN):
    return lax.dot_general(a, b, dims, precision=HIGHEST, preferred_element_type=jnp.float32)


def product(a, b, dims=NN):
    return lax.dot_general(a, b, dims, preferred_element_type=jnp.float32)


def halves(x):
    first = x.astype(jnp.bfloat16).astype(jnp.float32)
    return first, (x - first).astype(jnp.bfloat16).astype(jnp.float32)


def iota(shape, dim):
    return lax.broadcasted_iota(jnp.int32, shape, dim)


def kernel(
    tiles, depths,
    sub_in, ad_in, dis_in, block, coupling, tile_of, spot_of,
    sub_prev, sub_last, ad_prev, ad_last,
    s0, s1, s2, s3, adatoms, disorder,
    hx, hl, top, send, got, lhs, low_t, high, scat, red_a, red_b, ans, back, proj, rank_t, a1, a2,
    hx_s, hx_r, hl_s, hl_r, top_s, top_r, go_s, go_r, ra_s, ra_r, rb_s, rb_r, an_s, an_r,
):
    t = lax.axis_index("tile")
    d = lax.axis_index("depth")
    rows, layers = s0.shape[:2]
    count = tile_of.shape[1]
    slots = send.shape[2]
    sites = rows * 128
    states = [s0, s1, s2, s3]
    order_l = list(range(layers // 2, layers)) + list(range(layers // 2 - 1, -1, -1))

    def spread(x):
        return pl.ds(x, 8, stride=rows)

    barrier = pltpu.get_barrier_semaphore()

    def greet_tile(i):
        pl.semaphore_signal(
            barrier, inc=1, device_id=(lax.rem(t + i + 1, tiles), d), device_id_type=MESH
        )

    def greet_depth(i):
        pl.semaphore_signal(
            barrier, inc=1, device_id=(t, lax.rem(d + i + 1, depths)), device_id_type=MESH
        )

    each(tiles - 1, greet_tile)
    each(depths - 1, greet_depth)

    for side, (edge_t, edge_d) in enumerate(((0, 0), (tiles - 1, depths - 1))):

        @pl.when(t == edge_t)
        def _():
            hx[:, side] = jnp.zeros_like(hx[:, side])

        @pl.when(d == edge_d)
        def _():
            hl[:, side] = jnp.zeros_like(hl[:, side])

    def along_x(k, side, layer):
        step = 1 if side == 0 else -1
        return pltpu.make_async_remote_copy(
            src_ref=states[k].at[rows - 1 if side == 0 else 0, layer],
            dst_ref=hx.at[k, side, layer],
            send_sem=hx_s.at[k, side, layer], recv_sem=hx_r.at[k, side, layer],
            device_id=(lax.rem(t + step + tiles, tiles), d), device_id_type=MESH,
        )

    def along_l(k, side):
        step = 1 if side == 0 else -1
        return pltpu.make_async_remote_copy(
            src_ref=states[k].at[:, layers - 1 if side == 0 else 0],
            dst_ref=hl.at[k, side],
            send_sem=hl_s.at[k, side], recv_sem=hl_r.at[k, side],
            device_id=(t, lax.rem(d + step + depths, depths)), device_id_type=MESH,
        )

    send_x = (t < tiles - 1, t > 0)
    send_l = (d < depths - 1, d > 0)
    take_x = (t > 0, t < tiles - 1)
    take_l = (d > 0, d < depths - 1)

    def layer_start(k, layer):
        for side in range(2):
            pl.when(send_x[side])(along_x(k, side, layer).start)
        if layer == layers - 1:
            pl.when(send_l[0])(along_l(k, 0).start)
        if layer == 0:
            pl.when(send_l[1])(along_l(k, 1).start)

    def layer_wait(k, layer):
        if layer == 0:
            pl.when(take_l[0])(along_l(k, 0).wait_recv)
        if layer == layers - 1:
            pl.when(take_l[1])(along_l(k, 1).wait_recv)
        for side in range(2):
            pl.when(take_x[side])(along_x(k, side, layer).wait_recv)

    def halo_sent(k):
        for side in range(2):
            for layer in range(layers):
                pl.when(send_x[side])(along_x(k, side, layer).wait_send)
            pl.when(send_l[side])(along_l(k, side).wait_send)

    def top_copy(k, i):
        return pltpu.make_async_remote_copy(
            src_ref=top.at[k], dst_ref=top.at[k],
            send_sem=top_s.at[k, i], recv_sem=top_r.at[k],
            device_id=(t, i + 1), device_id_type=MESH,
        )

    def top_start(k):
        @pl.when(d == 0)
        def _():
            top[k] = states[k][:, 0]
            each(depths - 1, lambda i: top_copy(k, i).start())

    def top_wait(k):
        pl.when(d > 0)(lambda: top_copy(k, 0).wait_recv())

    def peer(i):
        return lax.rem(t + i + 1, tiles)

    def go_copy(other, to):
        return pltpu.make_async_remote_copy(
            src_ref=send.at[other], dst_ref=got.at[to],
            send_sem=go_s.at[other], recv_sem=go_r.at[to],
            device_id=(other, d), device_id_type=MESH,
        )

    def answer_copy(k, other, to):
        return pltpu.make_async_remote_copy(
            src_ref=ans.at[k, other], dst_ref=back.at[k, to],
            send_sem=an_s.at[k, other], recv_sem=an_r.at[k, to],
            device_id=(other, d), device_id_type=MESH,
        )

    def partial_copy(part, i):
        if part == 0:
            src, dst, ss, rs = scat.at[pl.ds(0, 8)], red_a, ra_s, ra_r
        else:
            src, dst, ss, rs = scat.at[pl.ds(8, 17)], red_b, rb_s, rb_r
        return pltpu.make_async_remote_copy(
            src_ref=src, dst_ref=dst.at[i], send_sem=ss, recv_sem=rs.at[i],
            device_id=(t, 0), device_id_type=MESH,
        )

    def reduce_wait(part):
        first, length = ((0, 8), (8, 17))[part]
        buffer = (red_a, red_b)[part]

        def add(i):
            partial_copy(part, i).wait_recv()
            scat[pl.ds(first, length)] += buffer[i]

        each(depths - 1, add)

    lane = iota((8, 8, 128), 2)
    sub = iota((8, 8, 128), 1)
    plus = iota((8, 8, 128), 0) % ORB < 2

    def stencil(k, l):
        layer_wait(k, l)
        field, out = states[k], states[k + 1]
        for x in range(rows):
            f = field[x, l]
            beside = field[x, l - 1] if l > 0 else hl[k, 0, x]
            beside += field[x, l + 1] if l < layers - 1 else hl[k, 1, x]
            beside += field[x - 1, l] if x > 0 else hx[k, 0, l]
            beside += field[x + 1, l] if x < rows - 1 else hx[k, 1, l]
            r = pltpu.roll(f, 1, 2)
            c = jnp.where(sub == 0, 0.0, pltpu.roll(r, 1, 1))
            beside += jnp.where(lane == 0, c, r)
            r = pltpu.roll(f, 127, 2)
            c = jnp.where(sub == 7, 0.0, pltpu.roll(r, 7, 1))
            beside += jnp.where(lane == 127, c, r)
            onsite = (disorder[x, l] - CHEMICAL)[None] * f - HOPPING * beside
            partner = jnp.concatenate([f[2:4], f[0:2], f[6:8], f[4:6]], axis=0)
            new = jnp.where(plus, onsite, -onsite) + PAIRING * partner
            if k > 0:
                new = 2.0 * new - states[k - 1][x, l]
            out[x, l] = new

    def hand_out(state, out):
        for x in range(rows):
            for l in range(layers):
                for q in range(8):
                    out[q % ORB, q // ORB, l, spread(x), :] = state[x, l, q]

    for x in range(rows):
        for l in order_l:
            for q in range(8):
                s0[x, l, q] = sub_in[q % ORB, q // ORB, l, spread(x), :]
    pl.semaphore_wait(barrier, tiles - 1 + depths - 1)
    for l in order_l:
        layer_start(0, l)
    top_start(0)
    for x in range(rows):
        for l in range(layers):
            disorder[x, l] = dis_in[l, spread(x), :]
    for v in range(2):
        adatoms[:, v * count : (v + 1) * count] = ad_in[:, v, :]

    b, c = block[...], coupling[...]
    cb = exact(c, b)
    proj[0:4] = c
    proj[4:8] = cb
    proj[8:12] = exact(cb, b)
    proj[12:16] = jnp.zeros((4, b.shape[0]), jnp.float32)
    pair1 = exact(c, c, NT)
    pair2 = exact(cb, c, NT)
    values = exact(proj[...], adatoms[...])
    values = jnp.concatenate([values[:, :count], values[:, count:]], axis=0)
    spot = spot_of[...].reshape(1, count)
    row = iota(values.shape, 0)
    values = jnp.where(row == LIVE, 1.0, values)
    values = jnp.where(row == HIGH, (spot // 128 % 8).astype(jnp.float32), values)
    values = jnp.where(row == LOW, (spot // 1024 * 128 + spot % 128).astype(jnp.float32), values)
    owner = (iota((tiles, count), 0) == tile_of[...]).astype(jnp.float32)
    earlier = (iota((count, count), 0) < iota((count, count), 1)).astype(jnp.float32)
    before = product(owner.astype(jnp.bfloat16), earlier.astype(jnp.bfloat16))
    rank = jnp.sum(owner * before, axis=0, keepdims=True).astype(jnp.int32)
    rank_t[...] = (iota((slots, count), 0) == rank).astype(jnp.float32).astype(jnp.bfloat16)
    parts = jnp.concatenate(halves(values), axis=0)

    def compact(g):
        chosen = [
            jnp.where(tile_of[...] == g * GROUP + i, parts, 0.0).astype(jnp.bfloat16)
            for i in range(GROUP)
        ]
        packed = product(jnp.concatenate(chosen, axis=0), rank_t[...], NT)
        for i in range(GROUP):
            at = i * 64
            send[g * GROUP + i] = packed[at : at + 32] + packed[at + 32 : at + 64]

    each(tiles // GROUP, compact)
    each(tiles - 1, lambda i: go_copy(peer(i), t).start())
    got[t] = send[t]

    for l in order_l:
        stencil(0, l)
        if l > 0:
            layer_start(1, l)
        else:
            pl.when(d > 0)(lambda: layer_start(1, 0))

    each(tiles - 1, lambda i: go_copy(peer(i), peer(i)).wait_recv())

    order = [v * 16 + j * 4 + o for j in range(STEPS) for v in range(2) for o in range(ORB)]
    order.append(LIVE)
    terms = len(order)
    wide = GROUP * slots

    def group(g):
        if tiles == GROUP:
            return slice(0, wide)
        return pl.ds(pl.multiple_of(g * wide, 128), wide)

    def scatter(g):
        data = jnp.concatenate([got[g * GROUP + i] for i in range(GROUP)], axis=1)
        first, second = halves(data)
        here = iota((8, wide), 0).astype(jnp.float32) == data[HIGH : HIGH + 1]
        high[:, group(g)] = here.astype(jnp.float32)
        low = iota((sites, wide), 0).astype(jnp.float32) == data[LOW : LOW + 1]
        low_t[:, group(g)] = low.astype(jnp.float32).astype(jnp.bfloat16)
        for at, q in enumerate(order):
            both = [jnp.where(here, part[q : q + 1], 0.0) for part in (first, second)]
            lhs[at * 16 : at * 16 + 16] = jnp.concatenate(both, axis=0).astype(jnp.bfloat16)
        total = product(lhs[...], low_t[:, group(g)], NT).reshape(terms, 2, 8, sites)
        total = total[:, 0] + total[:, 1]
        for x in range(rows):
            part = total[:, :, x * 128 : x * 128 + 128]
            if tiles == GROUP:
                scat[:, x] = part
            else:
                scat[:, x] += part

    if tiles > GROUP:
        scat[...] = jnp.zeros_like(scat)
    each(tiles // GROUP, scatter)

    @pl.when(d > 0)
    def _():
        partial_copy(0, d - 1).start()
        partial_copy(1, d - 1).start()

    def gather(k):
        top_wait(k)
        field = jnp.concatenate([top[k, x].reshape(64, 128) for x in range(rows)], axis=1)
        both = jnp.concatenate(halves(field), axis=0).astype(jnp.bfloat16)

        def one(g):
            found = product(both, low_t[:, group(g)])
            found = (found[:64] + found[64:]).reshape(8, 8, wide) * high[:, group(g)][None]
            found = jnp.sum(found, axis=1)
            for i in range(GROUP):
                ans[k, g * GROUP + i] = found[:, i * slots : (i + 1) * slots]

        each(tiles // GROUP, one)
        each(tiles - 1, lambda i: answer_copy(k, peer(i), t).start())
        back[k, t] = ans[k, t]

    def below(k):
        each(tiles - 1, lambda i: answer_copy(k, peer(i), peer(i)).wait_recv())
        first, second = halves(back[k].reshape(tiles * 8, slots))
        both = jnp.concatenate([first, second], axis=0).astype(jnp.bfloat16)
        found = product(both, rank_t[...])
        found = (found[: tiles * 8] + found[tiles * 8 :]).reshape(tiles, 8, count)
        found = jnp.sum(found * owner.reshape(tiles, 1, count), axis=0)
        return jnp.concatenate([found[0:4], found[4:8]], axis=1)

    ct = exact((iota(b.shape, 0) == iota(b.shape, 1)).astype(jnp.float32), c, NT)

    def adatom_part(k, vector):
        return exact(b, vector) + exact(ct, below(k))

    def mixed(pair, state, x):
        sums = []
        for v in range(2):
            for o in range(ORB):
                total = None
                for m in range(ORB):
                    term = pair[o : o + 1, m : m + 1] * state[x, 0, v * ORB + m]
                    total = term if total is None else total + term
                sums.append(total[None])
        return jnp.concatenate(sums, axis=0)

    gather(0)

    early = [l for l in order_l if l > 1]
    for l in early:
        stencil(1, l)
        layer_start(2, l)

    @pl.when(d == 0)
    def _():
        reduce_wait(0)
        for x in range(rows):
            s1[x, 0] += scat[0:8, x]
        layer_start(1, 0)

    top_start(1)

    for l in order_l:
        if l in early:
            continue
        stencil(1, l)
        if l > 0:
            layer_start(2, l)

    @pl.when(d == 0)
    def _():
        reduce_wait(1)
        for x in range(rows):
            extra = scat[8:16, x] + scat[24, x][None] * mixed(pair1, s0, x)
            s2[x, 0] += 2.0 * extra

    layer_start(2, 0)
    top_start(2)
    gather(1)
    a1[...] = adatom_part(0, adatoms[...])
    gather(2)
    hand_out(s2, sub_prev)
    for l in order_l:
        stencil(2, l)

    @pl.when(d == 0)
    def _():
        for x in range(rows):
            pairs = mixed(pair2, s0, x) + mixed(pair1, s1, x)
            extra = scat[16:24, x] + scat[24, x][None] * pairs
            s3[x, 0] += 2.0 * (2.0 * extra - scat[0:8, x])

    hand_out(s3, sub_last)

    def hand_adatoms(vectors, out):
        for v in range(2):
            out[:, v, :] = vectors[:, v * count : (v + 1) * count]

    a2[...] = 2.0 * adatom_part(1, a1[...]) - adatoms[...]
    hand_adatoms(a2[...], ad_prev)
    hand_adatoms(2.0 * adatom_part(2, a2[...]) - a1[...], ad_last)

    each(tiles - 1, lambda i: go_copy(peer(i), t).wait_send())
    for k in range(STEPS):
        halo_sent(k)
        each(tiles - 1, lambda i: answer_copy(k, peer(i), t).wait_send())

    @pl.when(d == 0)
    def _():
        for k in range(STEPS):
            each(depths - 1, lambda i: top_copy(k, i).wait_send())

    @pl.when(d > 0)
    def _():
        partial_copy(0, d - 1).wait_send()
        partial_copy(1, d - 1).wait_send()


def per_device(
    substrate_start, adatom_start, disorder, adatom_block, coupling, adatom_tile, adatom_spot
):
    tiles, depths = lax.axis_size("tile"), lax.axis_size("depth")
    count = adatom_spot.shape[0]
    orbs, vecs, layers, rows, cols = substrate_start.shape
    orba = adatom_block.shape[0]
    capacity = 2 * count // tiles
    slots = -(-capacity // 128) * 128
    f32 = jnp.float32

    def lined(x):
        lead = x.shape[:-2]
        n = len(lead)
        x = x.reshape(lead + (rows, 8, 128))
        x = x.transpose(tuple(range(n)) + (n + 1, n, n + 2))
        return x.reshape(lead + (8 * rows, 128))

    def unlined(x):
        lead = x.shape[:-2]
        n = len(lead)
        x = x.reshape(lead + (8, rows, 128))
        x = x.transpose(tuple(range(n)) + (n + 1, n, n + 2))
        return x.reshape(lead + (rows, cols))

    sites = lined(substrate_start)
    state = jax.ShapeDtypeStruct(sites.shape, f32)
    flat = jax.ShapeDtypeStruct(adatom_start.shape, f32)
    block_state = pltpu.VMEM((rows, layers, 8, 8, 128), f32)
    block_flat = pltpu.VMEM((orba, vecs * count), f32)
    wide = GROUP * slots
    dma = pltpu.SemaphoreType.DMA
    vmem = pl.BlockSpec(memory_space=pltpu.VMEM)
    s2, s3, a2, a3 = pl.pallas_call(
        functools.partial(kernel, tiles, depths),
        out_shape=(state, state, flat, flat),
        in_specs=[vmem] * 7,
        out_specs=(vmem,) * 4,
        scratch_shapes=[
            block_state, block_state, block_state, block_state,
            block_flat,
            pltpu.VMEM((rows, layers, 8, 128), f32),
            pltpu.VMEM((STEPS, 2, layers, 8, 8, 128), f32),
            pltpu.VMEM((STEPS, 2, rows, 8, 8, 128), f32),
            pltpu.VMEM((STEPS, rows, 8, 8, 128), f32),
            pltpu.VMEM((tiles, 32, slots), f32),
            pltpu.VMEM((tiles, 32, slots), f32),
            pltpu.VMEM((25 * 16, wide), jnp.bfloat16),
            pltpu.VMEM((rows * 128, tiles * slots), jnp.bfloat16),
            pltpu.VMEM((8, tiles * slots), f32),
            pltpu.VMEM((25, rows, 8, 128), f32),
            pltpu.VMEM((depths - 1, 8, rows, 8, 128), f32),
            pltpu.VMEM((depths - 1, 17, rows, 8, 128), f32),
            pltpu.VMEM((STEPS, tiles, 8, slots), f32),
            pltpu.VMEM((STEPS, tiles, 8, slots), f32),
            pltpu.VMEM((16, orba), f32),
            pltpu.VMEM((slots, count), jnp.bfloat16),
            block_flat, block_flat,
            dma((STEPS, 2, layers)), dma((STEPS, 2, layers)), dma((STEPS, 2)), dma((STEPS, 2)),
            dma((STEPS, depths - 1)), dma((STEPS,)),
            dma((tiles,)), dma((tiles,)),
            dma, dma((depths - 1,)), dma, dma((depths - 1,)),
            dma((STEPS, tiles)), dma((STEPS, tiles)),
        ],
        compiler_params=pltpu.CompilerParams(
            collective_id=0, has_side_effects=True, vmem_limit_bytes=56 * 1024 * 1024
        ),
    )(
        sites, adatom_start, lined(disorder), adatom_block, coupling,
        adatom_tile.reshape(1, count), adatom_spot,
    )
    return unlined(s2), unlined(s3), a2, a3


def solution(mesh):
    in_specs = (
        P(None, None, "depth", "tile", None),
        P(None, None, ("tile", "depth")),
        P("depth", "tile", None),
        P(),
        P(),
        P(("tile", "depth"), None),
        P(("tile", "depth")),
    )
    out_specs = (
        P(None, None, "depth", "tile", None),
        P(None, None, "depth", "tile", None),
        P(None, None, ("tile", "depth")),
        P(None, None, ("tile", "depth")),
    )
    return jax.shard_map(
        per_device, mesh=mesh, in_specs=in_specs, out_specs=out_specs, check_vma=False
    )
```

```python
import functools

import jax
import jax.numpy as jnp
from jax import lax
from jax.experimental import pallas as pl
from jax.experimental.pallas import tpu as pltpu
from jax.sharding import PartitionSpec as P

STEPS = 3
HOPPING = 0.12
CHEMICAL = 0.15
PAIRING = 0.3
ORB = 4
GROUP = 8
LIVE, HIGH, LOW = 12, 13, 14

MESH = pl.DeviceIdType.MESH
HIGHEST = lax.Precision.HIGHEST
NN = (((1,), (0,)), ((), ()))
NT = (((1,), (1,)), ((), ()))


def each(count, body):
    if count <= GROUP:
        for i in range(count):
            body(i)
    else:

        def run(i, carry):
            body(i)
            return carry

        lax.fori_loop(0, count, run, 0)


def exact(a, b, dims=NN):
    return lax.dot_general(a, b, dims, precision=HIGHEST, preferred_element_type=jnp.float32)


def product(a, b, dims=NN):
    return lax.dot_general(a, b, dims, preferred_element_type=jnp.float32)


def halves(x):
    first = x.astype(jnp.bfloat16).astype(jnp.float32)
    return first, (x - first).astype(jnp.bfloat16).astype(jnp.float32)


def iota(shape, dim):
    return lax.broadcasted_iota(jnp.int32, shape, dim)


def kernel(
    tiles, depths,
    sub_in, ad_in, dis_in, block, coupling, tile_of, spot_of,
    sub_prev, sub_last, ad_prev, ad_last,
    s0, s1, s2, s3, adatoms, disorder,
    hx, hl, top, send, got, lhs, low_t, high, scat, red_a, red_b, ans, back, proj, rank_t, a1, a2,
    hx_s, hx_r, hl_s, hl_r, top_s, top_r, go_s, go_r, ra_s, ra_r, rb_s, rb_r, an_s, an_r,
):
    t = lax.axis_index("tile")
    d = lax.axis_index("depth")
    rows, layers = s0.shape[:2]
    count = tile_of.shape[1]
    slots = send.shape[2]
    sites = rows * 128
    states = [s0, s1, s2, s3]
    order_l = list(range(layers // 2, layers)) + list(range(layers // 2 - 1, -1, -1))

    def spread(x):
        return pl.ds(x, 8, stride=rows)

    barrier = pltpu.get_barrier_semaphore()

    def greet_tile(i):
        pl.semaphore_signal(
            barrier, inc=1, device_id=(lax.rem(t + i + 1, tiles), d), device_id_type=MESH
        )

    def greet_depth(i):
        pl.semaphore_signal(
            barrier, inc=1, device_id=(t, lax.rem(d + i + 1, depths)), device_id_type=MESH
        )

    each(tiles - 1, greet_tile)
    each(depths - 1, greet_depth)

    for side, (edge_t, edge_d) in enumerate(((0, 0), (tiles - 1, depths - 1))):

        @pl.when(t == edge_t)
        def _():
            hx[:, side] = jnp.zeros_like(hx[:, side])

        @pl.when(d == edge_d)
        def _():
            hl[:, side] = jnp.zeros_like(hl[:, side])

    def along_x(k, side, layer):
        step = 1 if side == 0 else -1
        return pltpu.make_async_remote_copy(
            src_ref=states[k].at[rows - 1 if side == 0 else 0, layer],
            dst_ref=hx.at[k, side, layer],
            send_sem=hx_s.at[k, side, layer], recv_sem=hx_r.at[k, side, layer],
            device_id=(lax.rem(t + step + tiles, tiles), d), device_id_type=MESH,
        )

    def along_l(k, side):
        step = 1 if side == 0 else -1
        return pltpu.make_async_remote_copy(
            src_ref=states[k].at[:, layers - 1 if side == 0 else 0],
            dst_ref=hl.at[k, side],
            send_sem=hl_s.at[k, side], recv_sem=hl_r.at[k, side],
            device_id=(t, lax.rem(d + step + depths, depths)), device_id_type=MESH,
        )

    send_x = (t < tiles - 1, t > 0)
    send_l = (d < depths - 1, d > 0)
    take_x = (t > 0, t < tiles - 1)
    take_l = (d > 0, d < depths - 1)

    def layer_start(k, layer):
        for side in range(2):
            pl.when(send_x[side])(along_x(k, side, layer).start)
        if layer == layers - 1:
            pl.when(send_l[0])(along_l(k, 0).start)
        if layer == 0:
            pl.when(send_l[1])(along_l(k, 1).start)

    def layer_wait(k, layer):
        if layer == 0:
            pl.when(take_l[0])(along_l(k, 0).wait_recv)
        if layer == layers - 1:
            pl.when(take_l[1])(along_l(k, 1).wait_recv)
        for side in range(2):
            pl.when(take_x[side])(along_x(k, side, layer).wait_recv)

    def halo_sent(k):
        for side in range(2):
            for layer in range(layers):
                pl.when(send_x[side])(along_x(k, side, layer).wait_send)
            pl.when(send_l[side])(along_l(k, side).wait_send)

    def top_copy(k, i):
        return pltpu.make_async_remote_copy(
            src_ref=top.at[k], dst_ref=top.at[k],
            send_sem=top_s.at[k, i], recv_sem=top_r.at[k],
            device_id=(t, i + 1), device_id_type=MESH,
        )

    def top_start(k):
        @pl.when(d == 0)
        def _():
            top[k] = states[k][:, 0]
            each(depths - 1, lambda i: top_copy(k, i).start())

    def top_wait(k):
        pl.when(d > 0)(lambda: top_copy(k, 0).wait_recv())

    def peer(i):
        return lax.rem(t + i + 1, tiles)

    def go_copy(other, to):
        return pltpu.make_async_remote_copy(
            src_ref=send.at[other], dst_ref=got.at[to],
            send_sem=go_s.at[other], recv_sem=go_r.at[to],
            device_id=(other, d), device_id_type=MESH,
        )

    def answer_copy(k, other, to):
        return pltpu.make_async_remote_copy(
            src_ref=ans.at[k, other], dst_ref=back.at[k, to],
            send_sem=an_s.at[k, other], recv_sem=an_r.at[k, to],
            device_id=(other, d), device_id_type=MESH,
        )

    def partial_copy(part, i):
        if part == 0:
            src, dst, ss, rs = scat.at[pl.ds(0, 8)], red_a, ra_s, ra_r
        else:
            src, dst, ss, rs = scat.at[pl.ds(8, 17)], red_b, rb_s, rb_r
        return pltpu.make_async_remote_copy(
            src_ref=src, dst_ref=dst.at[i], send_sem=ss, recv_sem=rs.at[i],
            device_id=(t, 0), device_id_type=MESH,
        )

    def reduce_wait(part):
        first, length = ((0, 8), (8, 17))[part]
        buffer = (red_a, red_b)[part]

        def add(i):
            partial_copy(part, i).wait_recv()
            scat[pl.ds(first, length)] += buffer[i]

        each(depths - 1, add)

    lane = iota((8, 8, 128), 2)
    sub = iota((8, 8, 128), 1)
    plus = iota((8, 8, 128), 0) % ORB < 2

    def stencil(k, l):
        layer_wait(k, l)
        field, out = states[k], states[k + 1]
        for x in range(rows):
            f = field[x, l]
            beside = field[x, l - 1] if l > 0 else hl[k, 0, x]
            beside += field[x, l + 1] if l < layers - 1 else hl[k, 1, x]
            beside += field[x - 1, l] if x > 0 else hx[k, 0, l]
            beside += field[x + 1, l] if x < rows - 1 else hx[k, 1, l]
            r = pltpu.roll(f, 1, 2)
            c = jnp.where(sub == 0, 0.0, pltpu.roll(r, 1, 1))
            beside += jnp.where(lane == 0, c, r)
            r = pltpu.roll(f, 127, 2)
            c = jnp.where(sub == 7, 0.0, pltpu.roll(r, 7, 1))
            beside += jnp.where(lane == 127, c, r)
            onsite = (disorder[x, l] - CHEMICAL)[None] * f - HOPPING * beside
            partner = jnp.concatenate([f[2:4], f[0:2], f[6:8], f[4:6]], axis=0)
            new = jnp.where(plus, onsite, -onsite) + PAIRING * partner
            if k > 0:
                new = 2.0 * new - states[k - 1][x, l]
            out[x, l] = new

    def hand_out(state, out):
        for x in range(rows):
            for l in range(layers):
                for q in range(8):
                    out[q % ORB, q // ORB, l, spread(x), :] = state[x, l, q]

    for x in range(rows):
        for l in order_l:
            for q in range(8):
                s0[x, l, q] = sub_in[q % ORB, q // ORB, l, spread(x), :]
    owner = (iota((tiles, count), 0) == tile_of[...]).astype(jnp.float32)
    earlier = (iota((count, count), 0) < iota((count, count), 1)).astype(jnp.float32)
    before = product(owner.astype(jnp.bfloat16), earlier.astype(jnp.bfloat16))
    rank = jnp.sum(owner * before, axis=0, keepdims=True).astype(jnp.int32)
    rank_t[...] = (iota((slots, count), 0) == rank).astype(jnp.float32).astype(jnp.bfloat16)
    pl.semaphore_wait(barrier, tiles - 1 + depths - 1)
    for l in order_l:
        layer_start(0, l)
    top_start(0)
    for x in range(rows):
        for l in range(layers):
            disorder[x, l] = dis_in[l, spread(x), :]
    for v in range(2):
        adatoms[:, v * count : (v + 1) * count] = ad_in[:, v, :]

    b, c = block[...], coupling[...]
    cb = exact(c, b)
    proj[0:4] = c
    proj[4:8] = cb
    proj[8:12] = exact(cb, b)
    proj[12:16] = jnp.zeros((4, b.shape[0]), jnp.float32)
    pair1 = exact(c, c, NT)
    pair2 = exact(cb, c, NT)
    values = exact(proj[...], adatoms[...])
    values = jnp.concatenate([values[:, :count], values[:, count:]], axis=0)
    spot = spot_of[...].reshape(1, count)
    row = iota(values.shape, 0)
    values = jnp.where(row == LIVE, 1.0, values)
    values = jnp.where(row == HIGH, (spot // 128 % 8).astype(jnp.float32), values)
    values = jnp.where(row == LOW, (spot // 1024 * 128 + spot % 128).astype(jnp.float32), values)
    parts = jnp.concatenate(halves(values), axis=0)

    def compact(g):
        chosen = [
            jnp.where(tile_of[...] == g * GROUP + i, parts, 0.0).astype(jnp.bfloat16)
            for i in range(GROUP)
        ]
        packed = product(jnp.concatenate(chosen, axis=0), rank_t[...], NT)
        for i in range(GROUP):
            at = i * 64
            send[g * GROUP + i] = packed[at : at + 32] + packed[at + 32 : at + 64]

    each(tiles // GROUP, compact)
    each(tiles - 1, lambda i: go_copy(peer(i), t).start())
    got[t] = send[t]

    for l in order_l:
        stencil(0, l)
        if l > 0:
            layer_start(1, l)
        else:
            pl.when(d > 0)(lambda: layer_start(1, 0))

    each(tiles - 1, lambda i: go_copy(peer(i), peer(i)).wait_recv())

    order = [v * 16 + j * 4 + o for j in range(STEPS) for v in range(2) for o in range(ORB)]
    order.append(LIVE)
    terms = len(order)
    wide = GROUP * slots

    def group(g):
        if tiles == GROUP:
            return slice(0, wide)
        return pl.ds(pl.multiple_of(g * wide, 128), wide)

    def scatter(g):
        data = jnp.concatenate([got[g * GROUP + i] for i in range(GROUP)], axis=1)
        first, second = halves(data)
        here = iota((8, wide), 0).astype(jnp.float32) == data[HIGH : HIGH + 1]
        high[:, group(g)] = here.astype(jnp.float32)
        low = iota((sites, wide), 0).astype(jnp.float32) == data[LOW : LOW + 1]
        low_t[:, group(g)] = low.astype(jnp.float32).astype(jnp.bfloat16)
        for start, stop in ((0, 8), (8, terms)):
            for at in range(start, stop):
                q = order[at]
                both = [jnp.where(here, part[q : q + 1], 0.0) for part in (first, second)]
                lhs[at * 16 : at * 16 + 16] = jnp.concatenate(both, axis=0).astype(jnp.bfloat16)
            total = product(lhs[start * 16 : stop * 16], low_t[:, group(g)], NT)
            total = total.reshape(stop - start, 2, 8, sites)
            total = total[:, 0] + total[:, 1]
            for x in range(rows):
                part = total[:, :, x * 128 : x * 128 + 128]
                if tiles == GROUP:
                    scat[start:stop, x] = part
                else:
                    scat[start:stop, x] += part
            if tiles == GROUP:
                pl.when(d > 0)(partial_copy(start // 8, d - 1).start)

    if tiles > GROUP:
        scat[...] = jnp.zeros_like(scat)
    each(tiles // GROUP, scatter)
    if tiles > GROUP:
        for part in range(2):
            pl.when(d > 0)(partial_copy(part, d - 1).start)

    def gather(k):
        top_wait(k)
        field = jnp.concatenate([top[k, x].reshape(64, 128) for x in range(rows)], axis=1)
        both = jnp.concatenate(halves(field), axis=0).astype(jnp.bfloat16)

        def one(g):
            found = product(both, low_t[:, group(g)])
            found = (found[:64] + found[64:]).reshape(8, 8, wide) * high[:, group(g)][None]
            found = jnp.sum(found, axis=1)
            for i in range(GROUP):
                ans[k, g * GROUP + i] = found[:, i * slots : (i + 1) * slots]

        each(tiles // GROUP, one)
        each(tiles - 1, lambda i: answer_copy(k, peer(i), t).start())
        back[k, t] = ans[k, t]

    def below(k):
        each(tiles - 1, lambda i: answer_copy(k, peer(i), peer(i)).wait_recv())
        first, second = halves(back[k].reshape(tiles * 8, slots))
        both = jnp.concatenate([first, second], axis=0).astype(jnp.bfloat16)
        found = product(both, rank_t[...])
        found = (found[: tiles * 8] + found[tiles * 8 :]).reshape(tiles, 8, count)
        found = jnp.sum(found * owner.reshape(tiles, 1, count), axis=0)
        return jnp.concatenate([found[0:4], found[4:8]], axis=1)

    ct = exact((iota(b.shape, 0) == iota(b.shape, 1)).astype(jnp.float32), c, NT)

    def adatom_part(k, vector):
        return exact(b, vector) + exact(ct, below(k))

    def mixed(pair, state, x):
        sums = []
        for v in range(2):
            for o in range(ORB):
                total = None
                for m in range(ORB):
                    term = pair[o : o + 1, m : m + 1] * state[x, 0, v * ORB + m]
                    total = term if total is None else total + term
                sums.append(total[None])
        return jnp.concatenate(sums, axis=0)

    early = [l for l in order_l if l > 1]
    for l in early:
        stencil(1, l)
        layer_start(2, l)

    @pl.when(d == 0)
    def _():
        reduce_wait(0)
        for x in range(rows):
            s1[x, 0] += scat[0:8, x]
        layer_start(1, 0)

    top_start(1)
    gather(0)

    for l in order_l:
        if l in early:
            continue
        stencil(1, l)
        if l > 0:
            layer_start(2, l)

    @pl.when(d == 0)
    def _():
        reduce_wait(1)
        for x in range(rows):
            extra = scat[8:16, x] + scat[24, x][None] * mixed(pair1, s0, x)
            s2[x, 0] += 2.0 * extra

    layer_start(2, 0)
    top_start(2)
    gather(1)
    gather(2)
    hand_out(s2, sub_prev)
    for l in order_l:
        stencil(2, l)

    @pl.when(d == 0)
    def _():
        for x in range(rows):
            pairs = mixed(pair2, s0, x) + mixed(pair1, s1, x)
            extra = scat[16:24, x] + scat[24, x][None] * pairs
            s3[x, 0] += 2.0 * (2.0 * extra - scat[0:8, x])

    hand_out(s3, sub_last)

    def hand_adatoms(vectors, out):
        for v in range(2):
            out[:, v, :] = vectors[:, v * count : (v + 1) * count]

    a1[...] = adatom_part(0, adatoms[...])
    a2[...] = 2.0 * adatom_part(1, a1[...]) - adatoms[...]
    hand_adatoms(a2[...], ad_prev)
    hand_adatoms(2.0 * adatom_part(2, a2[...]) - a1[...], ad_last)

    each(tiles - 1, lambda i: go_copy(peer(i), t).wait_send())
    for k in range(STEPS):
        halo_sent(k)
        each(tiles - 1, lambda i: answer_copy(k, peer(i), t).wait_send())

    @pl.when(d == 0)
    def _():
        for k in range(STEPS):
            each(depths - 1, lambda i: top_copy(k, i).wait_send())

    @pl.when(d > 0)
    def _():
        partial_copy(0, d - 1).wait_send()
        partial_copy(1, d - 1).wait_send()


def settle(*arrays):
    n = len(arrays)
    chunks = 4

    def body(*refs):
        sems = refs[2 * n]
        copies = []
        for i in range(n):
            step = refs[i].shape[0] // chunks
            for j in range(chunks):
                at = pl.ds(j * step, step)
                copies.append(
                    pltpu.make_async_copy(refs[i].at[at], refs[n + i].at[at], sems.at[i, j])
                )
        for copy in copies:
            copy.start()
        for copy in copies:
            copy.wait()

    anywhere = pl.BlockSpec(memory_space=pl.ANY)
    return pl.pallas_call(
        body,
        out_shape=tuple(jax.ShapeDtypeStruct(x.shape, x.dtype) for x in arrays),
        in_specs=[anywhere] * n,
        out_specs=(anywhere,) * n,
        scratch_shapes=[pltpu.SemaphoreType.DMA((n, chunks))],
        compiler_params=pltpu.CompilerParams(vmem_limit_bytes=1 << 20),
    )(*arrays)


def per_device(
    substrate_start, adatom_start, disorder, adatom_block, coupling, adatom_tile, adatom_spot
):
    tiles, depths = lax.axis_size("tile"), lax.axis_size("depth")
    count = adatom_spot.shape[0]
    orbs, vecs, layers, rows, cols = substrate_start.shape
    orba = adatom_block.shape[0]
    capacity = 2 * count // tiles
    slots = -(-capacity // 128) * 128
    f32 = jnp.float32

    def lined(x):
        lead = x.shape[:-2]
        n = len(lead)
        x = x.reshape(lead + (rows, 8, 128))
        x = x.transpose(tuple(range(n)) + (n + 1, n, n + 2))
        return x.reshape(lead + (8 * rows, 128))

    def unlined(x):
        lead = x.shape[:-2]
        n = len(lead)
        x = x.reshape(lead + (8, rows, 128))
        x = x.transpose(tuple(range(n)) + (n + 1, n, n + 2))
        return x.reshape(lead + (rows, cols))

    sites = lined(substrate_start)
    state = jax.ShapeDtypeStruct(sites.shape, f32)
    flat = jax.ShapeDtypeStruct(adatom_start.shape, f32)
    block_state = pltpu.VMEM((rows, layers, 8, 8, 128), f32)
    block_flat = pltpu.VMEM((orba, vecs * count), f32)
    wide = GROUP * slots
    dma = pltpu.SemaphoreType.DMA
    vmem = pl.BlockSpec(memory_space=pltpu.VMEM)
    s2, s3, a2, a3 = pl.pallas_call(
        functools.partial(kernel, tiles, depths),
        out_shape=(state, state, flat, flat),
        in_specs=[vmem] * 7,
        out_specs=(vmem,) * 4,
        scratch_shapes=[
            block_state, block_state, block_state, block_state,
            block_flat,
            pltpu.VMEM((rows, layers, 8, 128), f32),
            pltpu.VMEM((STEPS, 2, layers, 8, 8, 128), f32),
            pltpu.VMEM((STEPS, 2, rows, 8, 8, 128), f32),
            pltpu.VMEM((STEPS, rows, 8, 8, 128), f32),
            pltpu.VMEM((tiles, 32, slots), f32),
            pltpu.VMEM((tiles, 32, slots), f32),
            pltpu.VMEM((25 * 16, wide), jnp.bfloat16),
            pltpu.VMEM((rows * 128, tiles * slots), jnp.bfloat16),
            pltpu.VMEM((8, tiles * slots), f32),
            pltpu.VMEM((25, rows, 8, 128), f32),
            pltpu.VMEM((depths - 1, 8, rows, 8, 128), f32),
            pltpu.VMEM((depths - 1, 17, rows, 8, 128), f32),
            pltpu.VMEM((STEPS, tiles, 8, slots), f32),
            pltpu.VMEM((STEPS, tiles, 8, slots), f32),
            pltpu.VMEM((16, orba), f32),
            pltpu.VMEM((slots, count), jnp.bfloat16),
            block_flat, block_flat,
            dma((STEPS, 2, layers)), dma((STEPS, 2, layers)), dma((STEPS, 2)), dma((STEPS, 2)),
            dma((STEPS, depths - 1)), dma((STEPS,)),
            dma((tiles,)), dma((tiles,)),
            dma, dma((depths - 1,)), dma, dma((depths - 1,)),
            dma((STEPS, tiles)), dma((STEPS, tiles)),
        ],
        compiler_params=pltpu.CompilerParams(
            collective_id=0, has_side_effects=True, vmem_limit_bytes=(56 if tiles > GROUP else 24) << 20
        ),
    )(
        sites, adatom_start, lined(disorder), adatom_block, coupling,
        adatom_tile.reshape(1, count), adatom_spot,
    )
    s2, s3, a2, a3 = settle(s2, s3, a2, a3)
    return unlined(s2), unlined(s3), a2, a3


def solution(mesh):
    in_specs = (
        P(None, None, "depth", "tile", None),
        P(None, None, ("tile", "depth")),
        P("depth", "tile", None),
        P(),
        P(),
        P(("tile", "depth"), None),
        P(("tile", "depth")),
    )
    out_specs = (
        P(None, None, "depth", "tile", None),
        P(None, None, "depth", "tile", None),
        P(None, None, ("tile", "depth")),
        P(None, None, ("tile", "depth")),
    )
    return jax.shard_map(
        per_device, mesh=mesh, in_specs=in_specs, out_specs=out_specs, check_vma=False
    )
```

```python
import functools

import jax
import jax.numpy as jnp
from jax import lax
from jax.experimental import pallas as pl
from jax.experimental.pallas import tpu as pltpu
from jax.sharding import PartitionSpec as P

STEPS = 3
HOPPING = 0.12
CHEMICAL = 0.15
PAIRING = 0.3
ORB = 4
GROUP = 8
HIGH, LOW = 8, 9

MESH = pl.DeviceIdType.MESH
HIGHEST = lax.Precision.HIGHEST
NN = (((1,), (0,)), ((), ()))
NT = (((1,), (1,)), ((), ()))


def each(count, body):
    if count <= GROUP:
        for i in range(count):
            body(i)
    else:

        def run(i, carry):
            body(i)
            return carry

        lax.fori_loop(0, count, run, 0)


def exact(a, b, dims=NN):
    return lax.dot_general(a, b, dims, precision=HIGHEST, preferred_element_type=jnp.float32)


def product(a, b, dims=NN):
    return lax.dot_general(a, b, dims, preferred_element_type=jnp.float32)


def halves(x):
    first = x.astype(jnp.bfloat16).astype(jnp.float32)
    return first, (x - first).astype(jnp.bfloat16).astype(jnp.float32)


def iota(shape, dim):
    return lax.broadcasted_iota(jnp.int32, shape, dim)


def kernel(
    tiles, depths,
    sub_hbm, ad_hbm, dis_hbm, block_hbm, coupling_hbm, tile_hbm, spot_hbm,
    sub_prev, sub_last, ad_prev, ad_last,
    s0, s1, s2, s3, adatoms, disorder,
    hx, hl, top, send, got, lhs, low_t, high, scat, red_a, red_b, ans, back, proj, rank_t, a1, a2,
    sub_in, ad_in, dis_in, block, coupling, tile_of, spot_of, in_s,
    hx_s, hx_r, hl_s, hl_r, top_s, top_r, go_s, go_r, ra_s, ra_r, rb_s, rb_r, an_s, an_r,
):
    t = lax.axis_index("tile")
    d = lax.axis_index("depth")
    rows, layers = s0.shape[:2]
    count = tile_of.shape[1]
    capacity = 2 * count // tiles
    slots = rank_t.shape[0]
    packed = send.shape[2] == 24
    each_wide = capacity if packed else slots
    sites = rows * 128
    states = [s0, s1, s2, s3]
    order_l = list(range(layers // 2, layers)) + list(range(layers // 2 - 1, -1, -1))

    def spread(x):
        return pl.ds(x, 8, stride=rows)

    fetches = [
        pltpu.make_async_copy(src, dst, in_s.at[i])
        for i, (src, dst) in enumerate((
            (tile_hbm, tile_of), (spot_hbm, spot_of), (coupling_hbm, coupling),
            (ad_hbm, ad_in), (block_hbm, block), (sub_hbm, sub_in), (dis_hbm, dis_in),
        ))
    ]
    for fetch in fetches:
        fetch.start()

    barrier = pltpu.get_barrier_semaphore()

    def greet_tile(i):
        pl.semaphore_signal(
            barrier, inc=1, device_id=(lax.rem(t + i + 1, tiles), d), device_id_type=MESH
        )

    def greet_depth(i):
        pl.semaphore_signal(
            barrier, inc=1, device_id=(t, lax.rem(d + i + 1, depths)), device_id_type=MESH
        )

    each(tiles - 1, greet_tile)
    each(depths - 1, greet_depth)

    for side, (edge_t, edge_d) in enumerate(((0, 0), (tiles - 1, depths - 1))):

        @pl.when(t == edge_t)
        def _():
            hx[:, side] = jnp.zeros_like(hx[:, side])

        @pl.when(d == edge_d)
        def _():
            hl[:, side] = jnp.zeros_like(hl[:, side])

    def along_x(k, side, layer):
        step = 1 if side == 0 else -1
        return pltpu.make_async_remote_copy(
            src_ref=states[k].at[rows - 1 if side == 0 else 0, layer],
            dst_ref=hx.at[k, side, layer],
            send_sem=hx_s.at[k, side, layer], recv_sem=hx_r.at[k, side, layer],
            device_id=(lax.rem(t + step + tiles, tiles), d), device_id_type=MESH,
        )

    def along_l(k, side):
        step = 1 if side == 0 else -1
        return pltpu.make_async_remote_copy(
            src_ref=states[k].at[:, layers - 1 if side == 0 else 0],
            dst_ref=hl.at[k, side],
            send_sem=hl_s.at[k, side], recv_sem=hl_r.at[k, side],
            device_id=(t, lax.rem(d + step + depths, depths)), device_id_type=MESH,
        )

    send_x = (t < tiles - 1, t > 0)
    send_l = (d < depths - 1, d > 0)
    take_x = (t > 0, t < tiles - 1)
    take_l = (d > 0, d < depths - 1)

    def layer_start(k, layer):
        for side in range(2):
            pl.when(send_x[side])(along_x(k, side, layer).start)
        if layer == layers - 1:
            pl.when(send_l[0])(along_l(k, 0).start)
        if layer == 0:
            pl.when(send_l[1])(along_l(k, 1).start)

    def layer_wait(k, layer):
        if layer == 0:
            pl.when(take_l[0])(along_l(k, 0).wait_recv)
        if layer == layers - 1:
            pl.when(take_l[1])(along_l(k, 1).wait_recv)
        for side in range(2):
            pl.when(take_x[side])(along_x(k, side, layer).wait_recv)

    def halo_sent(k):
        for side in range(2):
            for layer in range(layers):
                pl.when(send_x[side])(along_x(k, side, layer).wait_send)
            pl.when(send_l[side])(along_l(k, side).wait_send)

    def top_copy(k, i):
        return pltpu.make_async_remote_copy(
            src_ref=top.at[k], dst_ref=top.at[k],
            send_sem=top_s.at[k, i], recv_sem=top_r.at[k],
            device_id=(t, i + 1), device_id_type=MESH,
        )

    def top_start(k):
        @pl.when(d == 0)
        def _():
            top[k] = states[k][:, 0]
            each(depths - 1, lambda i: top_copy(k, i).start())

    def top_wait(k):
        pl.when(d > 0)(lambda: top_copy(k, 0).wait_recv())

    def peer(i):
        return lax.rem(t + i + 1, tiles)

    def go_copy(part, other, to):
        return pltpu.make_async_remote_copy(
            src_ref=send.at[part, other], dst_ref=got.at[part, to],
            send_sem=go_s.at[part, other], recv_sem=go_r.at[part, to],
            device_id=(other, d), device_id_type=MESH,
        )

    def answer_copy(k, other, to):
        return pltpu.make_async_remote_copy(
            src_ref=ans.at[k, other], dst_ref=back.at[k, to],
            send_sem=an_s.at[k, other], recv_sem=an_r.at[k, to],
            device_id=(other, d), device_id_type=MESH,
        )

    def partial_copy(part, i):
        if part == 0:
            src, dst, ss, rs = scat.at[pl.ds(0, 8)], red_a, ra_s, ra_r
        else:
            src, dst, ss, rs = scat.at[pl.ds(8, 17)], red_b, rb_s, rb_r
        return pltpu.make_async_remote_copy(
            src_ref=src, dst_ref=dst.at[i], send_sem=ss, recv_sem=rs.at[i],
            device_id=(t, 0), device_id_type=MESH,
        )

    def reduce_wait(part):
        first, length = ((0, 8), (8, 17))[part]
        buffer = (red_a, red_b)[part]

        def add(i):
            partial_copy(part, i).wait_recv()
            scat[pl.ds(first, length)] += buffer[i]

        each(depths - 1, add)

    lane = iota((8, 8, 128), 2)
    sub = iota((8, 8, 128), 1)
    plus = iota((8, 8, 128), 0) % ORB < 2

    def stencil(k, l):
        layer_wait(k, l)
        field, out = states[k], states[k + 1]
        for x in range(rows):
            f = field[x, l]
            beside = field[x, l - 1] if l > 0 else hl[k, 0, x]
            beside += field[x, l + 1] if l < layers - 1 else hl[k, 1, x]
            beside += field[x - 1, l] if x > 0 else hx[k, 0, l]
            beside += field[x + 1, l] if x < rows - 1 else hx[k, 1, l]
            r = pltpu.roll(f, 1, 2)
            c = jnp.where(sub == 0, 0.0, pltpu.roll(r, 1, 1))
            beside += jnp.where(lane == 0, c, r)
            r = pltpu.roll(f, 127, 2)
            c = jnp.where(sub == 7, 0.0, pltpu.roll(r, 7, 1))
            beside += jnp.where(lane == 127, c, r)
            onsite = (disorder[x, l] - CHEMICAL)[None] * f - HOPPING * beside
            partner = jnp.concatenate([f[2:4], f[0:2], f[6:8], f[4:6]], axis=0)
            new = jnp.where(plus, onsite, -onsite) + PAIRING * partner
            if k > 0:
                new = 2.0 * new - states[k - 1][x, l]
            out[x, l] = new

    def hand_out(state, out):
        for x in range(rows):
            for l in range(layers):
                for q in range(8):
                    out[q % ORB, q // ORB, l, spread(x), :] = state[x, l, q]

    half_lane = iota((8, 128), 1) < 64

    def compact(part, values):
        pieces = jnp.concatenate(halves(values), axis=0)

        def one(g):
            chosen = [
                jnp.where(tile_of[...] == g * GROUP + i, pieces, 0.0).astype(jnp.bfloat16)
                for i in range(GROUP)
            ]
            found = product(jnp.concatenate(chosen, axis=0), rank_t[...], NT)
            for i in range(GROUP):
                at = i * 32
                mine = found[at : at + 16] + found[at + 16 : at + 32]
                if packed:
                    send[part, g * GROUP + i, 0:16] = mine[:, :128]
                    tail = pltpu.roll(mine[8:16, 128:], 64, 1)
                    send[part, g * GROUP + i, 16:24] = jnp.where(
                        half_lane, mine[0:8, 128:], tail
                    )
                else:
                    send[part, g * GROUP + i] = mine

        each(tiles // GROUP, one)

    def compact_start(part):
        each(tiles - 1, lambda i: go_copy(part, peer(i), t).start())
        got[part, t] = send[part, t]

    fetches[0].wait()
    owner = (iota((tiles, count), 0) == tile_of[...]).astype(jnp.float32)
    earlier = (iota((count, count), 0) < iota((count, count), 1)).astype(jnp.float32)
    before = product(owner.astype(jnp.bfloat16), earlier.astype(jnp.bfloat16))
    rank = jnp.sum(owner * before, axis=0, keepdims=True).astype(jnp.int32)
    rank_t[...] = (iota((slots, count), 0) == rank).astype(jnp.float32).astype(jnp.bfloat16)

    for fetch in fetches[1:4]:
        fetch.wait()
    for v in range(2):
        adatoms[:, v * count : (v + 1) * count] = ad_in[:, v, :]
    c = coupling[...]
    values = exact(c, adatoms[...])
    spot = spot_of[...].reshape(1, count)
    row = iota((8, count), 0)
    where = jnp.where(row == 0, (spot // 128 % 8 + 1).astype(jnp.float32), 0.0)
    where = jnp.where(row == 1, (spot // 1024 * 128 + spot % 128).astype(jnp.float32), where)
    compact(0, jnp.concatenate([values[:, :count], values[:, count:], where], axis=0))

    for fetch in fetches[4:]:
        fetch.wait()
    for x in range(rows):
        for l in order_l:
            for q in range(8):
                s0[x, l, q] = sub_in[q % ORB, q // ORB, l, spread(x), :]
    pl.semaphore_wait(barrier, tiles - 1 + depths - 1)
    compact_start(0)
    for l in order_l:
        layer_start(0, l)
    top_start(0)

    b = block[...]
    cb = exact(c, b)
    proj[0:4] = cb
    proj[4:8] = exact(cb, b)
    pair1 = exact(c, c, NT)
    pair2 = exact(cb, c, NT)
    values = exact(proj[...], adatoms[...])
    compact(1, jnp.concatenate([values[:, :count], values[:, count:]], axis=0))
    compact_start(1)
    for x in range(rows):
        for l in range(layers):
            disorder[x, l] = dis_in[l, spread(x), :]

    wide = GROUP * each_wide

    def group(g):
        if tiles == GROUP:
            return slice(0, wide)
        return pl.ds(pl.multiple_of(g * wide, 128), wide)

    def arrived(part, g):
        blocks = [got[part, g * GROUP + i] for i in range(GROUP)]
        if packed:
            tails = []
            for i in range(0, GROUP, 2):
                one, two = blocks[i][16:24], blocks[i + 1][16:24]
                upper = jnp.where(half_lane, one, pltpu.roll(two, 64, 1))
                lower = jnp.where(half_lane, pltpu.roll(one, 64, 1), two)
                tails.append(jnp.concatenate([upper, lower], axis=0))
            blocks = [block_[0:16] for block_ in blocks] + tails
        return jnp.concatenate(blocks, axis=1)

    rows_b = [v * 8 + j * 4 + o for j in range(2) for v in range(2) for o in range(ORB)]

    def scatter(part, g):
        data = arrived(part, g)
        if part == 0:
            here = iota((8, wide), 0).astype(jnp.float32) + 1.0 == data[HIGH : HIGH + 1]
            high[:, group(g)] = here.astype(jnp.float32)
            low = iota((sites, wide), 0).astype(jnp.float32) == data[LOW : LOW + 1]
            low_t[:, group(g)] = low.astype(jnp.float32).astype(jnp.bfloat16)
        here = high[:, group(g)]
        start, terms = (0, 8) if part == 0 else (8, 17)
        first, second = halves(data)
        for at, q in enumerate(range(8) if part == 0 else rows_b):
            both = [here * piece[q : q + 1] for piece in (first, second)]
            lhs[at * 16 : at * 16 + 16] = jnp.concatenate(both, axis=0).astype(jnp.bfloat16)
        if part == 1:
            both = jnp.concatenate([here, jnp.zeros_like(here)], axis=0)
            lhs[256:272] = both.astype(jnp.bfloat16)
        total = product(lhs[: terms * 16], low_t[:, group(g)], NT)
        total = total.reshape(terms, 2, 8, sites)
        total = total[:, 0] + total[:, 1]
        for x in range(rows):
            mine = total[:, :, x * 128 : x * 128 + 128]
            if tiles == GROUP:
                scat[start : start + terms, x] = mine
            else:
                scat[start : start + terms, x] += mine

    if tiles > GROUP:
        scat[...] = jnp.zeros_like(scat)

    def scatter_all(part):
        each(tiles - 1, lambda i: go_copy(part, peer(i), peer(i)).wait_recv())
        each(tiles // GROUP, lambda g: scatter(part, g))
        pl.when(d > 0)(partial_copy(part, d - 1).start)

    scatter_all(0)
    for l in order_l:
        stencil(0, l)
        if l > 0:
            layer_start(1, l)

    @pl.when(d == 0)
    def _():
        reduce_wait(0)
        for x in range(rows):
            s1[x, 0] += scat[0:8, x]

    layer_start(1, 0)
    top_start(1)
    scatter_all(1)

    def gather(k):
        top_wait(k)
        field = jnp.concatenate([top[k, x].reshape(64, 128) for x in range(rows)], axis=1)
        both = jnp.concatenate(halves(field), axis=0).astype(jnp.bfloat16)

        def one(g):
            found = product(both, low_t[:, group(g)])
            found = (found[:64] + found[64:]).reshape(8, 8, wide) * high[:, group(g)][None]
            found = jnp.sum(found, axis=1)
            for i in range(GROUP):
                if packed:
                    ans[k, g * GROUP + i, 0:8] = found[:, i * 128 : i * 128 + 128]
                    at = (GROUP + i // 2) * 128
                    tail = found[:, at : at + 128]
                    ans[k, g * GROUP + i, 8:16] = tail if i % 2 == 0 else pltpu.roll(tail, 64, 1)
                else:
                    ans[k, g * GROUP + i] = found[:, i * slots : (i + 1) * slots]

        each(tiles // GROUP, one)
        each(tiles - 1, lambda i: answer_copy(k, peer(i), t).start())
        back[k, t] = ans[k, t]

    def below(k):
        each(tiles - 1, lambda i: answer_copy(k, peer(i), peer(i)).wait_recv())
        if packed:
            mine = [back[k, :, i : i + 8].reshape(tiles * 8, 128) for i in (0, 8)]
            mine = jnp.concatenate(mine, axis=1)
        else:
            mine = back[k].reshape(tiles * 8, slots)
        first, second = halves(mine)
        both = jnp.concatenate([first, second], axis=0).astype(jnp.bfloat16)
        found = product(both, rank_t[...])
        found = (found[: tiles * 8] + found[tiles * 8 :]).reshape(tiles, 8, count)
        found = jnp.sum(found * owner.reshape(tiles, 1, count), axis=0)
        return jnp.concatenate([found[0:4], found[4:8]], axis=1)

    ct = exact((iota(b.shape, 0) == iota(b.shape, 1)).astype(jnp.float32), c, NT)

    def adatom_part(k, vector):
        return exact(b, vector) + exact(ct, below(k))

    def mixed(pair, state, x):
        sums = []
        for v in range(2):
            for o in range(ORB):
                total = None
                for m in range(ORB):
                    term = pair[o : o + 1, m : m + 1] * state[x, 0, v * ORB + m]
                    total = term if total is None else total + term
                sums.append(total[None])
        return jnp.concatenate(sums, axis=0)

    gather(0)
    for l in order_l:
        stencil(1, l)
        if l > 0:
            layer_start(2, l)

    @pl.when(d == 0)
    def _():
        reduce_wait(1)
        for x in range(rows):
            extra = scat[8:16, x] + scat[24, x][None] * mixed(pair1, s0, x)
            s2[x, 0] += 2.0 * extra

    layer_start(2, 0)
    top_start(2)
    gather(1)
    hand_out(s2, sub_prev)
    gather(2)

    @pl.when(d == 0)
    def _():
        for x in range(rows):
            pairs = mixed(pair2, s0, x) + mixed(pair1, s1, x)
            extra = scat[16:24, x] + scat[24, x][None] * pairs
            scat[16:24, x] = 2.0 * (2.0 * extra - scat[0:8, x])

    for l in order_l:
        stencil(2, l)

    @pl.when(d == 0)
    def _():
        for x in range(rows):
            s3[x, 0] += scat[16:24, x]

    hand_out(s3, sub_last)

    def hand_adatoms(vectors, out):
        for v in range(2):
            out[:, v, :] = vectors[:, v * count : (v + 1) * count]

    a1[...] = adatom_part(0, adatoms[...])
    a2[...] = 2.0 * adatom_part(1, a1[...]) - adatoms[...]
    hand_adatoms(a2[...], ad_prev)
    hand_adatoms(2.0 * adatom_part(2, a2[...]) - a1[...], ad_last)

    for part in range(2):
        each(tiles - 1, lambda i: go_copy(part, peer(i), t).wait_send())
    for k in range(STEPS):
        halo_sent(k)
        each(tiles - 1, lambda i: answer_copy(k, peer(i), t).wait_send())

    @pl.when(d == 0)
    def _():
        for k in range(STEPS):
            each(depths - 1, lambda i: top_copy(k, i).wait_send())

    @pl.when(d > 0)
    def _():
        partial_copy(0, d - 1).wait_send()
        partial_copy(1, d - 1).wait_send()


def settle(*arrays):
    n = len(arrays)
    chunks = 4

    def body(*refs):
        sems = refs[2 * n]
        copies = []
        for i in range(n):
            step = refs[i].shape[0] // chunks
            for j in range(chunks):
                at = pl.ds(j * step, step)
                copies.append(
                    pltpu.make_async_copy(refs[i].at[at], refs[n + i].at[at], sems.at[i, j])
                )
        for copy in copies:
            copy.start()
        for copy in copies:
            copy.wait()

    anywhere = pl.BlockSpec(memory_space=pl.ANY)
    return pl.pallas_call(
        body,
        out_shape=tuple(jax.ShapeDtypeStruct(x.shape, x.dtype) for x in arrays),
        in_specs=[anywhere] * n,
        out_specs=(anywhere,) * n,
        scratch_shapes=[pltpu.SemaphoreType.DMA((n, chunks))],
        compiler_params=pltpu.CompilerParams(vmem_limit_bytes=56 << 20),
    )(*arrays)


def per_device(
    substrate_start, adatom_start, disorder, adatom_block, coupling, adatom_tile, adatom_spot
):
    tiles, depths = lax.axis_size("tile"), lax.axis_size("depth")
    count = adatom_spot.shape[0]
    orbs, vecs, layers, rows, cols = substrate_start.shape
    orba = adatom_block.shape[0]
    capacity = 2 * count // tiles
    slots = -(-capacity // 128) * 128
    f32 = jnp.float32

    def lined(x):
        lead = x.shape[:-2]
        n = len(lead)
        x = x.reshape(lead + (rows, 8, 128))
        x = x.transpose(tuple(range(n)) + (n + 1, n, n + 2))
        return x.reshape(lead + (8 * rows, 128))

    def unlined(x):
        lead = x.shape[:-2]
        n = len(lead)
        x = x.reshape(lead + (8, rows, 128))
        x = x.transpose(tuple(range(n)) + (n + 1, n, n + 2))
        return x.reshape(lead + (rows, cols))

    sites = lined(substrate_start)
    state = jax.ShapeDtypeStruct(sites.shape, f32)
    flat = jax.ShapeDtypeStruct(adatom_start.shape, f32)
    block_state = pltpu.VMEM((rows, layers, 8, 8, 128), f32)
    block_flat = pltpu.VMEM((orba, vecs * count), f32)
    packed = capacity == 192
    each_wide = capacity if packed else slots
    wide = GROUP * each_wide
    sent = (24, 128) if packed else (16, slots)
    answer = (16, 128) if packed else (8, slots)
    dma = pltpu.SemaphoreType.DMA
    vmem = pl.BlockSpec(memory_space=pltpu.VMEM)
    s2, s3, a2, a3 = pl.pallas_call(
        functools.partial(kernel, tiles, depths),
        out_shape=(state, state, flat, flat),
        in_specs=[pl.BlockSpec(memory_space=pltpu.HBM)] * 7,
        out_specs=(vmem,) * 4,
        scratch_shapes=[
            block_state, block_state, block_state, block_state,
            block_flat,
            pltpu.VMEM((rows, layers, 8, 128), f32),
            pltpu.VMEM((STEPS, 2, layers, 8, 8, 128), f32),
            pltpu.VMEM((STEPS, 2, rows, 8, 8, 128), f32),
            pltpu.VMEM((STEPS, rows, 8, 8, 128), f32),
            pltpu.VMEM((2, tiles) + sent, f32),
            pltpu.VMEM((2, tiles) + sent, f32),
            pltpu.VMEM((17 * 16, wide), jnp.bfloat16),
            pltpu.VMEM((rows * 128, tiles * each_wide), jnp.bfloat16),
            pltpu.VMEM((8, tiles * each_wide), f32),
            pltpu.VMEM((25, rows, 8, 128), f32),
            pltpu.VMEM((depths - 1, 8, rows, 8, 128), f32),
            pltpu.VMEM((depths - 1, 17, rows, 8, 128), f32),
            pltpu.VMEM((STEPS, tiles) + answer, f32),
            pltpu.VMEM((STEPS, tiles) + answer, f32),
            pltpu.VMEM((8, orba), f32),
            pltpu.VMEM((slots, count), jnp.bfloat16),
            block_flat, block_flat,
            pltpu.VMEM(sites.shape, f32),
            pltpu.VMEM(adatom_start.shape, f32),
            pltpu.VMEM((layers, 8 * rows, 128), f32),
            pltpu.VMEM(adatom_block.shape, f32),
            pltpu.VMEM(coupling.shape, f32),
            pltpu.VMEM((1, count), jnp.int32),
            pltpu.VMEM((count,), jnp.int32),
            dma((7,)),
            dma((STEPS, 2, layers)), dma((STEPS, 2, layers)), dma((STEPS, 2)), dma((STEPS, 2)),
            dma((STEPS, depths - 1)), dma((STEPS,)),
            dma((2, tiles)), dma((2, tiles)),
            dma, dma((depths - 1,)), dma, dma((depths - 1,)),
            dma((STEPS, tiles)), dma((STEPS, tiles)),
        ],
        compiler_params=pltpu.CompilerParams(
            collective_id=0, has_side_effects=True, vmem_limit_bytes=56 << 20
        ),
    )(
        sites, adatom_start, lined(disorder), adatom_block, coupling,
        adatom_tile.reshape(1, count), adatom_spot,
    )
    s2, s3, a2, a3 = settle(s2, s3, a2, a3)
    return unlined(s2), unlined(s3), a2, a3


def solution(mesh):
    in_specs = (
        P(None, None, "depth", "tile", None),
        P(None, None, ("tile", "depth")),
        P("depth", "tile", None),
        P(),
        P(),
        P(("tile", "depth"), None),
        P(("tile", "depth")),
    )
    out_specs = (
        P(None, None, "depth", "tile", None),
        P(None, None, "depth", "tile", None),
        P(None, None, ("tile", "depth")),
        P(None, None, ("tile", "depth")),
    )
    return jax.shard_map(
        per_device, mesh=mesh, in_specs=in_specs, out_specs=out_specs, check_vma=False
    )
```

```python
import functools

import jax
import jax.numpy as jnp
from jax import lax
from jax.experimental import pallas as pl
from jax.experimental.pallas import tpu as pltpu
from jax.sharding import PartitionSpec as P

STEPS = 3
HOPPING = 0.12
CHEMICAL = 0.15
PAIRING = 0.3
ORB = 4
GROUP = 8
HIGH, LOW = 8, 9

MESH = pl.DeviceIdType.MESH
HIGHEST = lax.Precision.HIGHEST
NN = (((1,), (0,)), ((), ()))
NT = (((1,), (1,)), ((), ()))


def each(count, body):
    if count <= GROUP:
        for i in range(count):
            body(i)
    else:

        def run(i, carry):
            body(i)
            return carry

        lax.fori_loop(0, count, run, 0)


def exact(a, b, dims=NN):
    return lax.dot_general(a, b, dims, precision=HIGHEST, preferred_element_type=jnp.float32)


def product(a, b, dims=NN):
    return lax.dot_general(a, b, dims, preferred_element_type=jnp.float32)


def halves(x):
    first = x.astype(jnp.bfloat16).astype(jnp.float32)
    return first, (x - first).astype(jnp.bfloat16).astype(jnp.float32)


def iota(shape, dim):
    return lax.broadcasted_iota(jnp.int32, shape, dim)


def kernel(
    tiles, depths,
    sub_hbm, ad_hbm, dis_hbm, block_hbm, coupling_hbm, tile_hbm, spot_hbm,
    sub_prev, sub_last, ad_prev, ad_last,
    s0, s1, s2, s3, adatoms, disorder,
    hx, hl, top, send, got, lhs, low_t, high, scat, red_a, red_b, ans, back, proj, rank_t, a1, a2,
    sub_in, ad_in, dis_in, block, coupling, tile_of, spot_of, in_s,
    hx_s, hx_r, hl_s, hl_r, top_s, top_r, go_s, go_r, ra_s, ra_r, rb_s, rb_r, an_s, an_r,
):
    t = lax.axis_index("tile")
    d = lax.axis_index("depth")
    rows, layers = s0.shape[:2]
    count = tile_of.shape[1]
    capacity = 2 * count // tiles
    slots = rank_t.shape[0]
    packed = send.shape[2] == 24
    each_wide = capacity if packed else slots
    sites = rows * 128
    states = [s0, s1, s2, s3]
    order_l = list(range(layers // 2, layers)) + list(range(layers // 2 - 1, -1, -1))

    def spread(x):
        return pl.ds(x, 8, stride=rows)

    fetches = [
        pltpu.make_async_copy(src, dst, in_s.at[i])
        for i, (src, dst) in enumerate((
            (sub_hbm, sub_in), (tile_hbm, tile_of), (spot_hbm, spot_of),
            (coupling_hbm, coupling), (ad_hbm, ad_in), (dis_hbm, dis_in), (block_hbm, block),
        ))
    ]
    for fetch in fetches:
        fetch.start()

    barrier = pltpu.get_barrier_semaphore()

    def greet_tile(i):
        pl.semaphore_signal(
            barrier, inc=1, device_id=(lax.rem(t + i + 1, tiles), d), device_id_type=MESH
        )

    def greet_depth(i):
        pl.semaphore_signal(
            barrier, inc=1, device_id=(t, lax.rem(d + i + 1, depths)), device_id_type=MESH
        )

    each(tiles - 1, greet_tile)
    each(depths - 1, greet_depth)

    for side, (edge_t, edge_d) in enumerate(((0, 0), (tiles - 1, depths - 1))):

        @pl.when(t == edge_t)
        def _():
            hx[:, side] = jnp.zeros_like(hx[:, side])

        @pl.when(d == edge_d)
        def _():
            hl[:, side] = jnp.zeros_like(hl[:, side])

    def along_x(k, side, layer):
        step = 1 if side == 0 else -1
        return pltpu.make_async_remote_copy(
            src_ref=states[k].at[rows - 1 if side == 0 else 0, layer],
            dst_ref=hx.at[k, side, layer],
            send_sem=hx_s.at[k, side, layer], recv_sem=hx_r.at[k, side, layer],
            device_id=(lax.rem(t + step + tiles, tiles), d), device_id_type=MESH,
        )

    def along_l(k, side):
        step = 1 if side == 0 else -1
        return pltpu.make_async_remote_copy(
            src_ref=states[k].at[:, layers - 1 if side == 0 else 0],
            dst_ref=hl.at[k, side],
            send_sem=hl_s.at[k, side], recv_sem=hl_r.at[k, side],
            device_id=(t, lax.rem(d + step + depths, depths)), device_id_type=MESH,
        )

    send_x = (t < tiles - 1, t > 0)
    send_l = (d < depths - 1, d > 0)
    take_x = (t > 0, t < tiles - 1)
    take_l = (d > 0, d < depths - 1)

    def layer_start(k, layer):
        for side in range(2):
            pl.when(send_x[side])(along_x(k, side, layer).start)
        if layer == layers - 1:
            pl.when(send_l[0])(along_l(k, 0).start)
        if layer == 0:
            pl.when(send_l[1])(along_l(k, 1).start)

    def layer_wait(k, layer):
        if layer == 0:
            pl.when(take_l[0])(along_l(k, 0).wait_recv)
        if layer == layers - 1:
            pl.when(take_l[1])(along_l(k, 1).wait_recv)
        for side in range(2):
            pl.when(take_x[side])(along_x(k, side, layer).wait_recv)

    def halo_sent(k):
        for side in range(2):
            for layer in range(layers):
                pl.when(send_x[side])(along_x(k, side, layer).wait_send)
            pl.when(send_l[side])(along_l(k, side).wait_send)

    def top_copy(k, i):
        return pltpu.make_async_remote_copy(
            src_ref=top.at[k], dst_ref=top.at[k],
            send_sem=top_s.at[k, i], recv_sem=top_r.at[k],
            device_id=(t, i + 1), device_id_type=MESH,
        )

    def top_start(k):
        @pl.when(d == 0)
        def _():
            top[k] = states[k][:, 0]
            each(depths - 1, lambda i: top_copy(k, i).start())

    def top_wait(k):
        pl.when(d > 0)(lambda: top_copy(k, 0).wait_recv())

    def peer(i):
        return lax.rem(t + i + 1, tiles)

    def go_copy(part, other, to):
        return pltpu.make_async_remote_copy(
            src_ref=send.at[part, other], dst_ref=got.at[part, to],
            send_sem=go_s.at[part, other], recv_sem=go_r.at[part, to],
            device_id=(other, d), device_id_type=MESH,
        )

    def answer_copy(k, other, to):
        return pltpu.make_async_remote_copy(
            src_ref=ans.at[k, other], dst_ref=back.at[k, to],
            send_sem=an_s.at[k, other], recv_sem=an_r.at[k, to],
            device_id=(other, d), device_id_type=MESH,
        )

    def partial_copy(part, i):
        if part == 0:
            src, dst, ss, rs = scat.at[pl.ds(0, 8)], red_a, ra_s, ra_r
        else:
            src, dst, ss, rs = scat.at[pl.ds(8, 17)], red_b, rb_s, rb_r
        return pltpu.make_async_remote_copy(
            src_ref=src, dst_ref=dst.at[i], send_sem=ss, recv_sem=rs.at[i],
            device_id=(t, 0), device_id_type=MESH,
        )

    def reduce_wait(part):
        first, length = ((0, 8), (8, 17))[part]
        buffer = (red_a, red_b)[part]

        def add(i):
            partial_copy(part, i).wait_recv()
            scat[pl.ds(first, length)] += buffer[i]

        each(depths - 1, add)

    lane = iota((8, 8, 128), 2)
    sub = iota((8, 8, 128), 1)
    plus = iota((8, 8, 128), 0) % ORB < 2

    def stencil(k, l):
        layer_wait(k, l)
        field, out = states[k], states[k + 1]
        for x in range(rows):
            f = field[x, l]
            beside = field[x, l - 1] if l > 0 else hl[k, 0, x]
            beside += field[x, l + 1] if l < layers - 1 else hl[k, 1, x]
            beside += field[x - 1, l] if x > 0 else hx[k, 0, l]
            beside += field[x + 1, l] if x < rows - 1 else hx[k, 1, l]
            r = pltpu.roll(f, 1, 2)
            c = jnp.where(sub == 0, 0.0, pltpu.roll(r, 1, 1))
            beside += jnp.where(lane == 0, c, r)
            r = pltpu.roll(f, 127, 2)
            c = jnp.where(sub == 7, 0.0, pltpu.roll(r, 7, 1))
            beside += jnp.where(lane == 127, c, r)
            onsite = (disorder[x, l] - CHEMICAL)[None] * f - HOPPING * beside
            partner = jnp.concatenate([f[2:4], f[0:2], f[6:8], f[4:6]], axis=0)
            new = jnp.where(plus, onsite, -onsite) + PAIRING * partner
            if k > 0:
                new = 2.0 * new - states[k - 1][x, l]
            out[x, l] = new

    def hand_out(state, out):
        for x in range(rows):
            for l in range(layers):
                for q in range(8):
                    out[q % ORB, q // ORB, l, spread(x), :] = state[x, l, q]

    half_lane = iota((8, 128), 1) < 64

    def compact(part, values):
        pieces = jnp.concatenate(halves(values), axis=0)

        def one(g):
            chosen = [
                jnp.where(tile_of[...] == g * GROUP + i, pieces, 0.0).astype(jnp.bfloat16)
                for i in range(GROUP)
            ]
            found = product(jnp.concatenate(chosen, axis=0), rank_t[...], NT)
            for i in range(GROUP):
                at = i * 32
                mine = found[at : at + 16] + found[at + 16 : at + 32]
                if packed:
                    send[part, g * GROUP + i, 0:16] = mine[:, :128]
                    tail = pltpu.roll(mine[8:16, 128:], 64, 1)
                    send[part, g * GROUP + i, 16:24] = jnp.where(
                        half_lane, mine[0:8, 128:], tail
                    )
                else:
                    send[part, g * GROUP + i] = mine

        each(tiles // GROUP, one)

    def compact_start(part):
        each(tiles - 1, lambda i: go_copy(part, peer(i), t).start())
        got[part, t] = send[part, t]

    for fetch in fetches[:1]:
        fetch.wait()
    for x in range(rows):
        for l in order_l:
            for q in range(8):
                s0[x, l, q] = sub_in[q % ORB, q // ORB, l, spread(x), :]
    pl.semaphore_wait(barrier, tiles - 1 + depths - 1)
    for l in order_l:
        layer_start(0, l)
    top_start(0)

    fetches[1].wait()
    owner = (iota((tiles, count), 0) == tile_of[...]).astype(jnp.float32)
    earlier = (iota((count, count), 0) < iota((count, count), 1)).astype(jnp.float32)
    before = product(owner.astype(jnp.bfloat16), earlier.astype(jnp.bfloat16))
    rank = jnp.sum(owner * before, axis=0, keepdims=True).astype(jnp.int32)
    rank_t[...] = (iota((slots, count), 0) == rank).astype(jnp.float32).astype(jnp.bfloat16)

    for fetch in fetches[2:5]:
        fetch.wait()
    for v in range(2):
        adatoms[:, v * count : (v + 1) * count] = ad_in[:, v, :]
    c = coupling[...]
    values = exact(c, adatoms[...])
    spot = spot_of[...].reshape(1, count)
    row = iota((8, count), 0)
    where = jnp.where(row == 0, (spot // 128 % 8 + 1).astype(jnp.float32), 0.0)
    where = jnp.where(row == 1, (spot // 1024 * 128 + spot % 128).astype(jnp.float32), where)
    compact(0, jnp.concatenate([values[:, :count], values[:, count:], where], axis=0))
    compact_start(0)
    for fetch in fetches[5:]:
        fetch.wait()
    for x in range(rows):
        for l in range(layers):
            disorder[x, l] = dis_in[l, spread(x), :]

    wide = GROUP * each_wide

    def group(g):
        if tiles == GROUP:
            return slice(0, wide)
        return pl.ds(pl.multiple_of(g * wide, 128), wide)

    def arrived(part, g):
        blocks = [got[part, g * GROUP + i] for i in range(GROUP)]
        if packed:
            tails = []
            for i in range(0, GROUP, 2):
                one, two = blocks[i][16:24], blocks[i + 1][16:24]
                upper = jnp.where(half_lane, one, pltpu.roll(two, 64, 1))
                lower = jnp.where(half_lane, pltpu.roll(one, 64, 1), two)
                tails.append(jnp.concatenate([upper, lower], axis=0))
            blocks = [block_[0:16] for block_ in blocks] + tails
        return jnp.concatenate(blocks, axis=1)

    rows_b = [v * 8 + j * 4 + o for j in range(2) for v in range(2) for o in range(ORB)]

    def scatter(part, g):
        data = arrived(part, g)
        if part == 0:
            here = iota((8, wide), 0).astype(jnp.float32) + 1.0 == data[HIGH : HIGH + 1]
            high[:, group(g)] = here.astype(jnp.float32)
            low = iota((sites, wide), 0).astype(jnp.float32) == data[LOW : LOW + 1]
            low_t[:, group(g)] = low.astype(jnp.float32).astype(jnp.bfloat16)
        here = high[:, group(g)]
        start, terms = (0, 8) if part == 0 else (8, 17)
        first, second = halves(data)
        for at, q in enumerate(range(8) if part == 0 else rows_b):
            both = [here * piece[q : q + 1] for piece in (first, second)]
            lhs[at * 16 : at * 16 + 16] = jnp.concatenate(both, axis=0).astype(jnp.bfloat16)
        if part == 1:
            both = jnp.concatenate([here, jnp.zeros_like(here)], axis=0)
            lhs[256:272] = both.astype(jnp.bfloat16)
        total = product(lhs[: terms * 16], low_t[:, group(g)], NT)
        total = total.reshape(terms, 2, 8, sites)
        total = total[:, 0] + total[:, 1]
        for x in range(rows):
            mine = total[:, :, x * 128 : x * 128 + 128]
            if tiles == GROUP:
                scat[start : start + terms, x] = mine
            else:
                scat[start : start + terms, x] += mine

    if tiles > GROUP:
        scat[...] = jnp.zeros_like(scat)

    def scatter_all(part):
        each(tiles - 1, lambda i: go_copy(part, peer(i), peer(i)).wait_recv())
        each(tiles // GROUP, lambda g: scatter(part, g))
        pl.when(d > 0)(partial_copy(part, d - 1).start)

    def gather(k):
        top_wait(k)
        field = jnp.concatenate([top[k, x].reshape(64, 128) for x in range(rows)], axis=1)
        both = jnp.concatenate(halves(field), axis=0).astype(jnp.bfloat16)

        def one(g):
            found = product(both, low_t[:, group(g)])
            found = (found[:64] + found[64:]).reshape(8, 8, wide) * high[:, group(g)][None]
            found = jnp.sum(found, axis=1)
            for i in range(GROUP):
                if packed:
                    ans[k, g * GROUP + i, 0:8] = found[:, i * 128 : i * 128 + 128]
                    at = (GROUP + i // 2) * 128
                    tail = found[:, at : at + 128]
                    ans[k, g * GROUP + i, 8:16] = tail if i % 2 == 0 else pltpu.roll(tail, 64, 1)
                else:
                    ans[k, g * GROUP + i] = found[:, i * slots : (i + 1) * slots]

        each(tiles // GROUP, one)
        each(tiles - 1, lambda i: answer_copy(k, peer(i), t).start())
        back[k, t] = ans[k, t]

    def below(k):
        each(tiles - 1, lambda i: answer_copy(k, peer(i), peer(i)).wait_recv())
        if packed:
            mine = [back[k, :, i : i + 8].reshape(tiles * 8, 128) for i in (0, 8)]
            mine = jnp.concatenate(mine, axis=1)
        else:
            mine = back[k].reshape(tiles * 8, slots)
        first, second = halves(mine)
        both = jnp.concatenate([first, second], axis=0).astype(jnp.bfloat16)
        found = product(both, rank_t[...])
        found = (found[: tiles * 8] + found[tiles * 8 :]).reshape(tiles, 8, count)
        found = jnp.sum(found * owner.reshape(tiles, 1, count), axis=0)
        return jnp.concatenate([found[0:4], found[4:8]], axis=1)

    def adatom_part(k, vector):
        return exact(b, vector) + exact(ct, below(k))

    def hand_adatoms(vectors, out):
        for v in range(2):
            out[:, v, :] = vectors[:, v * count : (v + 1) * count]

    def mixed(pair, state, x):
        sums = []
        for v in range(2):
            for o in range(ORB):
                total = None
                for m in range(ORB):
                    term = pair[o : o + 1, m : m + 1] * state[x, 0, v * ORB + m]
                    total = term if total is None else total + term
                sums.append(total[None])
        return jnp.concatenate(sums, axis=0)

    for l in order_l:
        if l == 0:
            scatter_all(0)
        stencil(0, l)
        if l > 0:
            layer_start(1, l)

    @pl.when(d == 0)
    def _():
        reduce_wait(0)
        for x in range(rows):
            s1[x, 0] += scat[0:8, x]

    layer_start(1, 0)
    top_start(1)

    b = block[...]
    cb = exact(c, b)
    proj[0:4] = cb
    proj[4:8] = exact(cb, b)
    pair1 = exact(c, c, NT)
    pair2 = exact(cb, c, NT)
    ct = exact((iota(b.shape, 0) == iota(b.shape, 1)).astype(jnp.float32), c, NT)
    values = exact(proj[...], adatoms[...])
    compact(1, jnp.concatenate([values[:, :count], values[:, count:]], axis=0))
    compact_start(1)

    between = [lambda: gather(0), lambda: gather(1), lambda: scatter_all(1)]
    for l in order_l:
        if l == 0:
            for work in between:
                work()
        stencil(1, l)
        if l > 0:
            layer_start(2, l)
            if between:
                between.pop(0)()

    @pl.when(d == 0)
    def _():
        reduce_wait(1)
        for x in range(rows):
            extra = scat[8:16, x] + scat[24, x][None] * mixed(pair1, s0, x)
            s2[x, 0] += 2.0 * extra

    layer_start(2, 0)
    top_start(2)
    hand_out(s2, sub_prev)
    a1[...] = adatom_part(0, adatoms[...])
    gather(2)

    @pl.when(d == 0)
    def _():
        for x in range(rows):
            pairs = mixed(pair2, s0, x) + mixed(pair1, s1, x)
            extra = scat[16:24, x] + scat[24, x][None] * pairs
            scat[16:24, x] = 2.0 * (2.0 * extra - scat[0:8, x])

    a2[...] = 2.0 * adatom_part(1, a1[...]) - adatoms[...]
    hand_adatoms(a2[...], ad_prev)
    for l in order_l:
        stencil(2, l)

    @pl.when(d == 0)
    def _():
        for x in range(rows):
            s3[x, 0] += scat[16:24, x]

    hand_out(s3, sub_last)

    hand_adatoms(2.0 * adatom_part(2, a2[...]) - a1[...], ad_last)

    for part in range(2):
        each(tiles - 1, lambda i: go_copy(part, peer(i), t).wait_send())
    for k in range(STEPS):
        halo_sent(k)
        each(tiles - 1, lambda i: answer_copy(k, peer(i), t).wait_send())

    @pl.when(d == 0)
    def _():
        for k in range(STEPS):
            each(depths - 1, lambda i: top_copy(k, i).wait_send())

    @pl.when(d > 0)
    def _():
        partial_copy(0, d - 1).wait_send()
        partial_copy(1, d - 1).wait_send()


def settle(*arrays):
    n = len(arrays)
    chunks = 2

    def body(*refs):
        held, sems = refs[2 * n : 3 * n], refs[3 * n]
        copies, leaves = [], []
        for i in range(n):
            step = refs[i].shape[0] // chunks
            for j in range(chunks):
                at = pl.ds(j * step, step)
                copies.append(
                    pltpu.make_async_copy(refs[i].at[at], held[i].at[at], sems.at[0, i, j])
                )
                leaves.append(
                    pltpu.make_async_copy(held[i].at[at], refs[n + i].at[at], sems.at[1, i, j])
                )
        for copy in copies:
            copy.start()
        for copy, leave in zip(copies, leaves):
            copy.wait()
            leave.start()
        for leave in leaves:
            leave.wait()

    anywhere = pl.BlockSpec(memory_space=pl.ANY)
    return pl.pallas_call(
        body,
        out_shape=tuple(jax.ShapeDtypeStruct(x.shape, x.dtype) for x in arrays),
        in_specs=[anywhere] * n,
        out_specs=(anywhere,) * n,
        scratch_shapes=[pltpu.VMEM(x.shape, x.dtype) for x in arrays]
        + [pltpu.SemaphoreType.DMA((2, n, chunks))],
        compiler_params=pltpu.CompilerParams(vmem_limit_bytes=56 << 20),
    )(*arrays)


def per_device(
    substrate_start, adatom_start, disorder, adatom_block, coupling, adatom_tile, adatom_spot
):
    tiles, depths = lax.axis_size("tile"), lax.axis_size("depth")
    count = adatom_spot.shape[0]
    orbs, vecs, layers, rows, cols = substrate_start.shape
    orba = adatom_block.shape[0]
    capacity = 2 * count // tiles
    slots = -(-capacity // 128) * 128
    f32 = jnp.float32

    def lined(x):
        lead = x.shape[:-2]
        n = len(lead)
        x = x.reshape(lead + (rows, 8, 128))
        x = x.transpose(tuple(range(n)) + (n + 1, n, n + 2))
        return x.reshape(lead + (8 * rows, 128))

    def unlined(x):
        lead = x.shape[:-2]
        n = len(lead)
        x = x.reshape(lead + (8, rows, 128))
        x = x.transpose(tuple(range(n)) + (n + 1, n, n + 2))
        return x.reshape(lead + (rows, cols))

    sites = lined(substrate_start)
    state = jax.ShapeDtypeStruct(sites.shape, f32)
    flat = jax.ShapeDtypeStruct(adatom_start.shape, f32)
    block_state = pltpu.VMEM((rows, layers, 8, 8, 128), f32)
    block_flat = pltpu.VMEM((orba, vecs * count), f32)
    packed = capacity == 192
    each_wide = capacity if packed else slots
    wide = GROUP * each_wide
    sent = (24, 128) if packed else (16, slots)
    answer = (16, 128) if packed else (8, slots)
    dma = pltpu.SemaphoreType.DMA
    vmem = pl.BlockSpec(memory_space=pltpu.VMEM)
    s2, s3, a2, a3 = pl.pallas_call(
        functools.partial(kernel, tiles, depths),
        out_shape=(state, state, flat, flat),
        in_specs=[pl.BlockSpec(memory_space=pltpu.HBM)] * 7,
        out_specs=(vmem,) * 4,
        scratch_shapes=[
            block_state, block_state, block_state, block_state,
            block_flat,
            pltpu.VMEM((rows, layers, 8, 128), f32),
            pltpu.VMEM((STEPS, 2, layers, 8, 8, 128), f32),
            pltpu.VMEM((STEPS, 2, rows, 8, 8, 128), f32),
            pltpu.VMEM((STEPS, rows, 8, 8, 128), f32),
            pltpu.VMEM((2, tiles) + sent, f32),
            pltpu.VMEM((2, tiles) + sent, f32),
            pltpu.VMEM((17 * 16, wide), jnp.bfloat16),
            pltpu.VMEM((rows * 128, tiles * each_wide), jnp.bfloat16),
            pltpu.VMEM((8, tiles * each_wide), f32),
            pltpu.VMEM((25, rows, 8, 128), f32),
            pltpu.VMEM((depths - 1, 8, rows, 8, 128), f32),
            pltpu.VMEM((depths - 1, 17, rows, 8, 128), f32),
            pltpu.VMEM((STEPS, tiles) + answer, f32),
            pltpu.VMEM((STEPS, tiles) + answer, f32),
            pltpu.VMEM((8, orba), f32),
            pltpu.VMEM((slots, count), jnp.bfloat16),
            block_flat, block_flat,
            pltpu.VMEM(sites.shape, f32),
            pltpu.VMEM(adatom_start.shape, f32),
            pltpu.VMEM((layers, 8 * rows, 128), f32),
            pltpu.VMEM(adatom_block.shape, f32),
            pltpu.VMEM(coupling.shape, f32),
            pltpu.VMEM((1, count), jnp.int32),
            pltpu.VMEM((count,), jnp.int32),
            dma((7,)),
            dma((STEPS, 2, layers)), dma((STEPS, 2, layers)), dma((STEPS, 2)), dma((STEPS, 2)),
            dma((STEPS, depths - 1)), dma((STEPS,)),
            dma((2, tiles)), dma((2, tiles)),
            dma, dma((depths - 1,)), dma, dma((depths - 1,)),
            dma((STEPS, tiles)), dma((STEPS, tiles)),
        ],
        compiler_params=pltpu.CompilerParams(
            collective_id=0, has_side_effects=True, vmem_limit_bytes=56 << 20
        ),
    )(
        sites, adatom_start, lined(disorder), adatom_block, coupling,
        adatom_tile.reshape(1, count), adatom_spot,
    )
    s2, s3, a2, a3 = settle(s2, s3, a2, a3)
    return unlined(s2), unlined(s3), a2, a3


def solution(mesh):
    in_specs = (
        P(None, None, "depth", "tile", None),
        P(None, None, ("tile", "depth")),
        P("depth", "tile", None),
        P(),
        P(),
        P(("tile", "depth"), None),
        P(("tile", "depth")),
    )
    out_specs = (
        P(None, None, "depth", "tile", None),
        P(None, None, "depth", "tile", None),
        P(None, None, ("tile", "depth")),
        P(None, None, ("tile", "depth")),
    )
    return jax.shard_map(
        per_device, mesh=mesh, in_specs=in_specs, out_specs=out_specs, check_vma=False
    )
```

```python
import functools

import jax
import jax.numpy as jnp
from jax import lax
from jax.experimental import pallas as pl
from jax.experimental.pallas import tpu as pltpu
from jax.sharding import PartitionSpec as P

STEPS = 3
HOPPING = 0.12
CHEMICAL = 0.15
PAIRING = 0.3
ORB = 4
GROUP = 8
HIGH, LOW = 8, 9

MESH = pl.DeviceIdType.MESH
HIGHEST = lax.Precision.HIGHEST
NN = (((1,), (0,)), ((), ()))
NT = (((1,), (1,)), ((), ()))


def each(count, body):
    if count <= GROUP:
        for i in range(count):
            body(i)
    else:

        def run(i, carry):
            body(i)
            return carry

        lax.fori_loop(0, count, run, 0)


def exact(a, b, dims=NN):
    return lax.dot_general(a, b, dims, precision=HIGHEST, preferred_element_type=jnp.float32)


def product(a, b, dims=NN):
    return lax.dot_general(a, b, dims, preferred_element_type=jnp.float32)


def halves(x):
    first = x.astype(jnp.bfloat16).astype(jnp.float32)
    return first, (x - first).astype(jnp.bfloat16).astype(jnp.float32)


def iota(shape, dim):
    return lax.broadcasted_iota(jnp.int32, shape, dim)


def kernel(
    tiles, depths,
    sub_hbm, ad_hbm, dis_hbm, block_hbm, coupling_hbm, tile_hbm, spot_hbm,
    sub_prev, sub_last, ad_prev, ad_last,
    s0, s1, s2, s3, adatoms, disorder,
    hx, hl, top, send, got, lhs, low_t, high, scat, red_a, red_b, ans, back, proj, rank_t, a1, a2,
    sub_in, ad_in, dis_in, block, coupling, tile_of, spot_of, in_s,
    hx_s, hx_r, hl_s, hl_r, top_s, top_r, go_s, go_r, ra_s, ra_r, rb_s, rb_r, an_s, an_r,
):
    t = lax.axis_index("tile")
    d = lax.axis_index("depth")
    rows, layers = s0.shape[:2]
    count = tile_of.shape[1]
    capacity = 2 * count // tiles
    slots = rank_t.shape[0]
    packed = send.shape[2] == 24
    each_wide = capacity if packed else slots
    sites = rows * 128
    states = [s0, s1, s2, s3]
    order_l = list(range(layers // 2, layers)) + list(range(layers // 2 - 1, -1, -1))

    def spread(x):
        return pl.ds(x, 8, stride=rows)

    fetches = [
        pltpu.make_async_copy(src, dst, in_s.at[i])
        for i, (src, dst) in enumerate((
            (tile_hbm, tile_of), (sub_hbm, sub_in), (spot_hbm, spot_of),
            (coupling_hbm, coupling), (ad_hbm, ad_in), (dis_hbm, dis_in), (block_hbm, block),
        ))
    ]
    for fetch in fetches:
        fetch.start()

    barrier = pltpu.get_barrier_semaphore()

    def greet_tile(i):
        pl.semaphore_signal(
            barrier, inc=1, device_id=(lax.rem(t + i + 1, tiles), d), device_id_type=MESH
        )

    def greet_depth(i):
        pl.semaphore_signal(
            barrier, inc=1, device_id=(t, lax.rem(d + i + 1, depths)), device_id_type=MESH
        )

    each(tiles - 1, greet_tile)
    each(depths - 1, greet_depth)

    for side, (edge_t, edge_d) in enumerate(((0, 0), (tiles - 1, depths - 1))):

        @pl.when(t == edge_t)
        def _():
            hx[:, side] = jnp.zeros_like(hx[:, side])

        @pl.when(d == edge_d)
        def _():
            hl[:, side] = jnp.zeros_like(hl[:, side])

    def along_x(k, side, layer):
        step = 1 if side == 0 else -1
        return pltpu.make_async_remote_copy(
            src_ref=states[k].at[rows - 1 if side == 0 else 0, layer],
            dst_ref=hx.at[k, side, layer],
            send_sem=hx_s.at[k, side, layer], recv_sem=hx_r.at[k, side, layer],
            device_id=(lax.rem(t + step + tiles, tiles), d), device_id_type=MESH,
        )

    def along_l(k, side):
        step = 1 if side == 0 else -1
        return pltpu.make_async_remote_copy(
            src_ref=states[k].at[:, layers - 1 if side == 0 else 0],
            dst_ref=hl.at[k, side],
            send_sem=hl_s.at[k, side], recv_sem=hl_r.at[k, side],
            device_id=(t, lax.rem(d + step + depths, depths)), device_id_type=MESH,
        )

    send_x = (t < tiles - 1, t > 0)
    send_l = (d < depths - 1, d > 0)
    take_x = (t > 0, t < tiles - 1)
    take_l = (d > 0, d < depths - 1)

    def layer_start(k, layer):
        for side in range(2):
            pl.when(send_x[side])(along_x(k, side, layer).start)
        if layer == layers - 1:
            pl.when(send_l[0])(along_l(k, 0).start)
        if layer == 0:
            pl.when(send_l[1])(along_l(k, 1).start)

    def layer_wait(k, layer):
        if layer == 0:
            pl.when(take_l[0])(along_l(k, 0).wait_recv)
        if layer == layers - 1:
            pl.when(take_l[1])(along_l(k, 1).wait_recv)
        for side in range(2):
            pl.when(take_x[side])(along_x(k, side, layer).wait_recv)

    def halo_sent(k):
        for side in range(2):
            for layer in range(layers):
                pl.when(send_x[side])(along_x(k, side, layer).wait_send)
            pl.when(send_l[side])(along_l(k, side).wait_send)

    def top_copy(k, i):
        return pltpu.make_async_remote_copy(
            src_ref=top.at[k], dst_ref=top.at[k],
            send_sem=top_s.at[k, i], recv_sem=top_r.at[k],
            device_id=(t, i + 1), device_id_type=MESH,
        )

    def top_start(k):
        @pl.when(d == 0)
        def _():
            top[k] = states[k][:, 0]
            each(depths - 1, lambda i: top_copy(k, i).start())

    def top_wait(k):
        pl.when(d > 0)(lambda: top_copy(k, 0).wait_recv())

    def peer(i):
        return lax.rem(t + i + 1, tiles)

    def go_copy(part, other, to):
        return pltpu.make_async_remote_copy(
            src_ref=send.at[part, other], dst_ref=got.at[part, to],
            send_sem=go_s.at[part, other], recv_sem=go_r.at[part, to],
            device_id=(other, d), device_id_type=MESH,
        )

    def answer_copy(k, other, to):
        return pltpu.make_async_remote_copy(
            src_ref=ans.at[k, other], dst_ref=back.at[k, to],
            send_sem=an_s.at[k, other], recv_sem=an_r.at[k, to],
            device_id=(other, d), device_id_type=MESH,
        )

    def partial_copy(part, i):
        if part == 0:
            src, dst, ss, rs = scat.at[pl.ds(0, 8)], red_a, ra_s, ra_r
        else:
            src, dst, ss, rs = scat.at[pl.ds(8, 17)], red_b, rb_s, rb_r
        return pltpu.make_async_remote_copy(
            src_ref=src, dst_ref=dst.at[i], send_sem=ss, recv_sem=rs.at[i],
            device_id=(t, 0), device_id_type=MESH,
        )

    def reduce_wait(part):
        first, length = ((0, 8), (8, 17))[part]
        buffer = (red_a, red_b)[part]

        def add(i):
            partial_copy(part, i).wait_recv()
            scat[pl.ds(first, length)] += buffer[i]

        each(depths - 1, add)

    lane = iota((8, 8, 128), 2)
    sub = iota((8, 8, 128), 1)
    plus = iota((8, 8, 128), 0) % ORB < 2

    def stencil(k, l):
        layer_wait(k, l)
        field, out = states[k], states[k + 1]
        for x in range(rows):
            f = field[x, l]
            beside = field[x, l - 1] if l > 0 else hl[k, 0, x]
            beside += field[x, l + 1] if l < layers - 1 else hl[k, 1, x]
            beside += field[x - 1, l] if x > 0 else hx[k, 0, l]
            beside += field[x + 1, l] if x < rows - 1 else hx[k, 1, l]
            r = pltpu.roll(f, 1, 2)
            c = jnp.where(sub == 0, 0.0, pltpu.roll(r, 1, 1))
            beside += jnp.where(lane == 0, c, r)
            r = pltpu.roll(f, 127, 2)
            c = jnp.where(sub == 7, 0.0, pltpu.roll(r, 7, 1))
            beside += jnp.where(lane == 127, c, r)
            onsite = (disorder[x, l] - CHEMICAL)[None] * f - HOPPING * beside
            partner = jnp.concatenate([f[2:4], f[0:2], f[6:8], f[4:6]], axis=0)
            new = jnp.where(plus, onsite, -onsite) + PAIRING * partner
            if k > 0:
                new = 2.0 * new - states[k - 1][x, l]
            out[x, l] = new

    def hand_out(state, out):
        for x in range(rows):
            for l in range(layers):
                for q in range(8):
                    out[q % ORB, q // ORB, l, spread(x), :] = state[x, l, q]

    half_lane = iota((8, 128), 1) < 64

    def compact(part, values):
        pieces = jnp.concatenate(halves(values), axis=0)

        def one(g):
            chosen = [
                jnp.where(tile_of[...] == g * GROUP + i, pieces, 0.0).astype(jnp.bfloat16)
                for i in range(GROUP)
            ]
            found = product(jnp.concatenate(chosen, axis=0), rank_t[...], NT)
            for i in range(GROUP):
                at = i * 32
                mine = found[at : at + 16] + found[at + 16 : at + 32]
                if packed:
                    send[part, g * GROUP + i, 0:16] = mine[:, :128]
                    tail = pltpu.roll(mine[8:16, 128:], 64, 1)
                    send[part, g * GROUP + i, 16:24] = jnp.where(
                        half_lane, mine[0:8, 128:], tail
                    )
                else:
                    send[part, g * GROUP + i] = mine

        each(tiles // GROUP, one)

    def compact_start(part):
        each(tiles - 1, lambda i: go_copy(part, peer(i), t).start())
        got[part, t] = send[part, t]

    fetches[0].wait()
    owner = (iota((tiles, count), 0) == tile_of[...]).astype(jnp.float32)
    earlier = (iota((count, count), 0) < iota((count, count), 1)).astype(jnp.float32)
    before = product(owner.astype(jnp.bfloat16), earlier.astype(jnp.bfloat16))
    rank = jnp.sum(owner * before, axis=0, keepdims=True).astype(jnp.int32)
    rank_t[...] = (iota((slots, count), 0) == rank).astype(jnp.float32).astype(jnp.bfloat16)

    fetches[1].wait()
    for x in range(rows):
        for l in order_l:
            for q in range(8):
                s0[x, l, q] = sub_in[q % ORB, q // ORB, l, spread(x), :]
    pl.semaphore_wait(barrier, tiles - 1 + depths - 1)
    for l in order_l[: layers // 2]:
        layer_start(0, l)


    for fetch in fetches[2:5]:
        fetch.wait()
    for v in range(2):
        adatoms[:, v * count : (v + 1) * count] = ad_in[:, v, :]
    c = coupling[...]
    values = exact(c, adatoms[...])
    spot = spot_of[...].reshape(1, count)
    row = iota((8, count), 0)
    where = jnp.where(row == 0, (spot // 128 % 8 + 1).astype(jnp.float32), 0.0)
    where = jnp.where(row == 1, (spot // 1024 * 128 + spot % 128).astype(jnp.float32), where)
    compact(0, jnp.concatenate([values[:, :count], values[:, count:], where], axis=0))
    compact_start(0)
    for l in order_l[layers // 2 :]:
        layer_start(0, l)
    top_start(0)
    for fetch in fetches[5:]:
        fetch.wait()
    for x in range(rows):
        for l in range(layers):
            disorder[x, l] = dis_in[l, spread(x), :]

    wide = GROUP * each_wide

    def group(g):
        if tiles == GROUP:
            return slice(0, wide)
        return pl.ds(pl.multiple_of(g * wide, 128), wide)

    def arrived(part, g):
        blocks = [got[part, g * GROUP + i] for i in range(GROUP)]
        if packed:
            tails = []
            for i in range(0, GROUP, 2):
                one, two = blocks[i][16:24], blocks[i + 1][16:24]
                upper = jnp.where(half_lane, one, pltpu.roll(two, 64, 1))
                lower = jnp.where(half_lane, pltpu.roll(one, 64, 1), two)
                tails.append(jnp.concatenate([upper, lower], axis=0))
            blocks = [block_[0:16] for block_ in blocks] + tails
        return jnp.concatenate(blocks, axis=1)

    rows_b = [v * 8 + j * 4 + o for j in range(2) for v in range(2) for o in range(ORB)]

    def scatter(part, g):
        data = arrived(part, g)
        if part == 0:
            here = iota((8, wide), 0).astype(jnp.float32) + 1.0 == data[HIGH : HIGH + 1]
            high[:, group(g)] = here.astype(jnp.float32)
            low = iota((sites, wide), 0).astype(jnp.float32) == data[LOW : LOW + 1]
            low_t[:, group(g)] = low.astype(jnp.float32).astype(jnp.bfloat16)
        here = high[:, group(g)]
        start, terms = (0, 8) if part == 0 else (8, 17)
        first, second = halves(data)
        for at, q in enumerate(range(8) if part == 0 else rows_b):
            both = [here * piece[q : q + 1] for piece in (first, second)]
            lhs[at * 16 : at * 16 + 16] = jnp.concatenate(both, axis=0).astype(jnp.bfloat16)
        if part == 1:
            both = jnp.concatenate([here, jnp.zeros_like(here)], axis=0)
            lhs[256:272] = both.astype(jnp.bfloat16)
        total = product(lhs[: terms * 16], low_t[:, group(g)], NT)
        total = total.reshape(terms, 2, 8, sites)
        total = total[:, 0] + total[:, 1]
        for x in range(rows):
            mine = total[:, :, x * 128 : x * 128 + 128]
            if tiles == GROUP:
                scat[start : start + terms, x] = mine
            else:
                scat[start : start + terms, x] += mine

    if tiles > GROUP:
        scat[...] = jnp.zeros_like(scat)

    def scatter_all(part):
        each(tiles - 1, lambda i: go_copy(part, peer(i), peer(i)).wait_recv())
        each(tiles // GROUP, lambda g: scatter(part, g))
        pl.when(d > 0)(partial_copy(part, d - 1).start)

    def gather(k):
        top_wait(k)
        field = jnp.concatenate([top[k, x].reshape(64, 128) for x in range(rows)], axis=1)
        both = jnp.concatenate(halves(field), axis=0).astype(jnp.bfloat16)

        def one(g):
            found = product(both, low_t[:, group(g)])
            found = (found[:64] + found[64:]).reshape(8, 8, wide) * high[:, group(g)][None]
            found = jnp.sum(found, axis=1)
            for i in range(GROUP):
                if packed:
                    ans[k, g * GROUP + i, 0:8] = found[:, i * 128 : i * 128 + 128]
                    at = (GROUP + i // 2) * 128
                    tail = found[:, at : at + 128]
                    ans[k, g * GROUP + i, 8:16] = tail if i % 2 == 0 else pltpu.roll(tail, 64, 1)
                else:
                    ans[k, g * GROUP + i] = found[:, i * slots : (i + 1) * slots]

        each(tiles // GROUP, one)
        each(tiles - 1, lambda i: answer_copy(k, peer(i), t).start())
        back[k, t] = ans[k, t]

    def below(k):
        each(tiles - 1, lambda i: answer_copy(k, peer(i), peer(i)).wait_recv())
        if packed:
            mine = [back[k, :, i : i + 8].reshape(tiles * 8, 128) for i in (0, 8)]
            mine = jnp.concatenate(mine, axis=1)
        else:
            mine = back[k].reshape(tiles * 8, slots)
        first, second = halves(mine)
        both = jnp.concatenate([first, second], axis=0).astype(jnp.bfloat16)
        found = product(both, rank_t[...])
        found = (found[: tiles * 8] + found[tiles * 8 :]).reshape(tiles, 8, count)
        found = jnp.sum(found * owner.reshape(tiles, 1, count), axis=0)
        return jnp.concatenate([found[0:4], found[4:8]], axis=1)

    def adatom_part(k, vector):
        return exact(b, vector) + exact(ct, below(k))

    def hand_adatoms(vectors, out):
        for v in range(2):
            out[:, v, :] = vectors[:, v * count : (v + 1) * count]

    def mixed(pair, state, x):
        sums = []
        for v in range(2):
            for o in range(ORB):
                total = None
                for m in range(ORB):
                    term = pair[o : o + 1, m : m + 1] * state[x, 0, v * ORB + m]
                    total = term if total is None else total + term
                sums.append(total[None])
        return jnp.concatenate(sums, axis=0)

    b = block[...]
    cb = exact(c, b)
    proj[0:4] = cb
    proj[4:8] = exact(cb, b)
    pair1 = exact(c, c, NT)
    pair2 = exact(cb, c, NT)
    ct = exact((iota(b.shape, 0) == iota(b.shape, 1)).astype(jnp.float32), c, NT)
    values = exact(proj[...], adatoms[...])
    compact(1, jnp.concatenate([values[:, :count], values[:, count:]], axis=0))
    compact_start(1)

    scatter_all(0)
    for l in order_l:
        stencil(0, l)
        if l > 0:
            layer_start(1, l)

    @pl.when(d == 0)
    def _():
        reduce_wait(0)
        for x in range(rows):
            s1[x, 0] += scat[0:8, x]

    top_start(1)
    layer_start(1, 0)

    scatter_all(1)
    gather(0)
    gather(1)
    for l in order_l:
        stencil(1, l)
        if l > 0:
            layer_start(2, l)

    @pl.when(d == 0)
    def _():
        reduce_wait(1)
        for x in range(rows):
            extra = scat[8:16, x] + scat[24, x][None] * mixed(pair1, s0, x)
            s2[x, 0] += 2.0 * extra

    top_start(2)
    layer_start(2, 0)
    hand_out(s2, sub_prev)
    a1[...] = adatom_part(0, adatoms[...])
    gather(2)

    @pl.when(d == 0)
    def _():
        for x in range(rows):
            pairs = mixed(pair2, s0, x) + mixed(pair1, s1, x)
            extra = scat[16:24, x] + scat[24, x][None] * pairs
            scat[16:24, x] = 2.0 * (2.0 * extra - scat[0:8, x])

    a2[...] = 2.0 * adatom_part(1, a1[...]) - adatoms[...]
    hand_adatoms(a2[...], ad_prev)
    for l in order_l:
        stencil(2, l)

    @pl.when(d == 0)
    def _():
        for x in range(rows):
            s3[x, 0] += scat[16:24, x]

    hand_out(s3, sub_last)

    hand_adatoms(2.0 * adatom_part(2, a2[...]) - a1[...], ad_last)

    for part in range(2):
        each(tiles - 1, lambda i: go_copy(part, peer(i), t).wait_send())
    for k in range(STEPS):
        halo_sent(k)
        each(tiles - 1, lambda i: answer_copy(k, peer(i), t).wait_send())

    @pl.when(d == 0)
    def _():
        for k in range(STEPS):
            each(depths - 1, lambda i: top_copy(k, i).wait_send())

    @pl.when(d > 0)
    def _():
        partial_copy(0, d - 1).wait_send()
        partial_copy(1, d - 1).wait_send()


def settle(*arrays):
    n = len(arrays)
    chunks = 2

    def body(*refs):
        held, sems = refs[2 * n : 3 * n], refs[3 * n]
        copies, leaves = [], []
        for i in range(n):
            step = refs[i].shape[0] // chunks
            for j in range(chunks):
                at = pl.ds(j * step, step)
                copies.append(
                    pltpu.make_async_copy(refs[i].at[at], held[i].at[at], sems.at[0, i, j])
                )
                leaves.append(
                    pltpu.make_async_copy(held[i].at[at], refs[n + i].at[at], sems.at[1, i, j])
                )
        for copy in copies:
            copy.start()
        for copy, leave in zip(copies, leaves):
            copy.wait()
            leave.start()
        for leave in leaves:
            leave.wait()

    anywhere = pl.BlockSpec(memory_space=pl.ANY)
    return pl.pallas_call(
        body,
        out_shape=tuple(jax.ShapeDtypeStruct(x.shape, x.dtype) for x in arrays),
        in_specs=[anywhere] * n,
        out_specs=(anywhere,) * n,
        scratch_shapes=[pltpu.VMEM(x.shape, x.dtype) for x in arrays]
        + [pltpu.SemaphoreType.DMA((2, n, chunks))],
        compiler_params=pltpu.CompilerParams(vmem_limit_bytes=56 << 20),
    )(*arrays)


def per_device(
    substrate_start, adatom_start, disorder, adatom_block, coupling, adatom_tile, adatom_spot
):
    tiles, depths = lax.axis_size("tile"), lax.axis_size("depth")
    count = adatom_spot.shape[0]
    orbs, vecs, layers, rows, cols = substrate_start.shape
    orba = adatom_block.shape[0]
    capacity = 2 * count // tiles
    slots = -(-capacity // 128) * 128
    f32 = jnp.float32

    def lined(x):
        lead = x.shape[:-2]
        n = len(lead)
        x = x.reshape(lead + (rows, 8, 128))
        x = x.transpose(tuple(range(n)) + (n + 1, n, n + 2))
        return x.reshape(lead + (8 * rows, 128))

    def unlined(x):
        lead = x.shape[:-2]
        n = len(lead)
        x = x.reshape(lead + (8, rows, 128))
        x = x.transpose(tuple(range(n)) + (n + 1, n, n + 2))
        return x.reshape(lead + (rows, cols))

    sites = lined(substrate_start)
    state = jax.ShapeDtypeStruct(sites.shape, f32)
    flat = jax.ShapeDtypeStruct(adatom_start.shape, f32)
    block_state = pltpu.VMEM((rows, layers, 8, 8, 128), f32)
    block_flat = pltpu.VMEM((orba, vecs * count), f32)
    packed = capacity == 192
    each_wide = capacity if packed else slots
    wide = GROUP * each_wide
    sent = (24, 128) if packed else (16, slots)
    answer = (16, 128) if packed else (8, slots)
    dma = pltpu.SemaphoreType.DMA
    vmem = pl.BlockSpec(memory_space=pltpu.VMEM)
    s2, s3, a2, a3 = pl.pallas_call(
        functools.partial(kernel, tiles, depths),
        out_shape=(state, state, flat, flat),
        in_specs=[pl.BlockSpec(memory_space=pltpu.HBM)] * 7,
        out_specs=(vmem,) * 4,
        scratch_shapes=[
            block_state, block_state, block_state, block_state,
            block_flat,
            pltpu.VMEM((rows, layers, 8, 128), f32),
            pltpu.VMEM((STEPS, 2, layers, 8, 8, 128), f32),
            pltpu.VMEM((STEPS, 2, rows, 8, 8, 128), f32),
            pltpu.VMEM((STEPS, rows, 8, 8, 128), f32),
            pltpu.VMEM((2, tiles) + sent, f32),
            pltpu.VMEM((2, tiles) + sent, f32),
            pltpu.VMEM((17 * 16, wide), jnp.bfloat16),
            pltpu.VMEM((rows * 128, tiles * each_wide), jnp.bfloat16),
            pltpu.VMEM((8, tiles * each_wide), f32),
            pltpu.VMEM((25, rows, 8, 128), f32),
            pltpu.VMEM((depths - 1, 8, rows, 8, 128), f32),
            pltpu.VMEM((depths - 1, 17, rows, 8, 128), f32),
            pltpu.VMEM((STEPS, tiles) + answer, f32),
            pltpu.VMEM((STEPS, tiles) + answer, f32),
            pltpu.VMEM((8, orba), f32),
            pltpu.VMEM((slots, count), jnp.bfloat16),
            block_flat, block_flat,
            pltpu.VMEM(sites.shape, f32),
            pltpu.VMEM(adatom_start.shape, f32),
            pltpu.VMEM((layers, 8 * rows, 128), f32),
            pltpu.VMEM(adatom_block.shape, f32),
            pltpu.VMEM(coupling.shape, f32),
            pltpu.VMEM((1, count), jnp.int32),
            pltpu.VMEM((count,), jnp.int32),
            dma((7,)),
            dma((STEPS, 2, layers)), dma((STEPS, 2, layers)), dma((STEPS, 2)), dma((STEPS, 2)),
            dma((STEPS, depths - 1)), dma((STEPS,)),
            dma((2, tiles)), dma((2, tiles)),
            dma, dma((depths - 1,)), dma, dma((depths - 1,)),
            dma((STEPS, tiles)), dma((STEPS, tiles)),
        ],
        compiler_params=pltpu.CompilerParams(
            collective_id=0, has_side_effects=True, vmem_limit_bytes=56 << 20
        ),
    )(
        sites, adatom_start, lined(disorder), adatom_block, coupling,
        adatom_tile.reshape(1, count), adatom_spot,
    )
    s2, s3, a2, a3 = settle(s2, s3, a2, a3)
    return unlined(s2), unlined(s3), a2, a3


def solution(mesh):
    in_specs = (
        P(None, None, "depth", "tile", None),
        P(None, None, ("tile", "depth")),
        P("depth", "tile", None),
        P(),
        P(),
        P(("tile", "depth"), None),
        P(("tile", "depth")),
    )
    out_specs = (
        P(None, None, "depth", "tile", None),
        P(None, None, "depth", "tile", None),
        P(None, None, ("tile", "depth")),
        P(None, None, ("tile", "depth")),
    )
    return jax.shard_map(
        per_device, mesh=mesh, in_specs=in_specs, out_specs=out_specs, check_vma=False
    )
```

```python
import functools

import jax
import jax.numpy as jnp
from jax import lax
from jax.experimental import pallas as pl
from jax.experimental.pallas import tpu as pltpu
from jax.sharding import PartitionSpec as P

STEPS = 3
HOPPING = 0.12
CHEMICAL = 0.15
PAIRING = 0.3
ORB = 4
GROUP = 8
HIGH, LOW = 8, 9

MESH = pl.DeviceIdType.MESH
HIGHEST = lax.Precision.HIGHEST
NN = (((1,), (0,)), ((), ()))
NT = (((1,), (1,)), ((), ()))


def each(count, body):
    if count <= GROUP:
        for i in range(count):
            body(i)
    else:

        def run(i, carry):
            body(i)
            return carry

        lax.fori_loop(0, count, run, 0)


def exact(a, b, dims=NN):
    return lax.dot_general(a, b, dims, precision=HIGHEST, preferred_element_type=jnp.float32)


def product(a, b, dims=NN):
    return lax.dot_general(a, b, dims, preferred_element_type=jnp.float32)


def halves(x):
    first = x.astype(jnp.bfloat16).astype(jnp.float32)
    return first, (x - first).astype(jnp.bfloat16).astype(jnp.float32)


def iota(shape, dim):
    return lax.broadcasted_iota(jnp.int32, shape, dim)


def kernel(
    tiles, depths,
    sub_hbm, ad_hbm, dis_hbm, block_hbm, coupling_hbm, tile_hbm, spot_hbm,
    sub_prev, sub_last, ad_prev, ad_last,
    s0, s1, s2, s3, adatoms, disorder,
    hx, hl, top, send, got, lhs, low_t, high, scat, red_a, red_b, ans, back, proj, rank_t, a1, a2,
    sub_in, ad_in, dis_in, block, coupling, tile_of, spot_of, in_s,
    hx_s, hx_r, hl_s, hl_r, top_s, top_r, go_s, go_r, ra_s, ra_r, rb_s, rb_r, an_s, an_r,
):
    t = lax.axis_index("tile")
    d = lax.axis_index("depth")
    rows, layers = s0.shape[:2]
    count = tile_of.shape[1]
    capacity = 2 * count // tiles
    slots = rank_t.shape[0]
    packed = send.shape[2] == 24
    each_wide = capacity if packed else slots
    sites = rows * 128
    states = [s0, s1, s2, s3]
    order_l = [1, 0] + list(range(2, layers)) if layers > 1 else [0]

    def spread(x):
        return pl.ds(x, 8, stride=rows)

    fetches = [
        pltpu.make_async_copy(src, dst, in_s.at[i])
        for i, (src, dst) in enumerate((
            (tile_hbm, tile_of), (sub_hbm, sub_in), (spot_hbm, spot_of),
            (coupling_hbm, coupling), (ad_hbm, ad_in), (dis_hbm, dis_in), (block_hbm, block),
        ))
    ]
    for fetch in fetches:
        fetch.start()

    barrier = pltpu.get_barrier_semaphore()

    def greet_tile(i):
        pl.semaphore_signal(
            barrier, inc=1, device_id=(lax.rem(t + i + 1, tiles), d), device_id_type=MESH
        )

    def greet_depth(i):
        pl.semaphore_signal(
            barrier, inc=1, device_id=(t, lax.rem(d + i + 1, depths)), device_id_type=MESH
        )

    each(tiles - 1, greet_tile)
    each(depths - 1, greet_depth)

    for side, (edge_t, edge_d) in enumerate(((0, 0), (tiles - 1, depths - 1))):

        @pl.when(t == edge_t)
        def _():
            hx[:, side] = jnp.zeros_like(hx[:, side])

        @pl.when(d == edge_d)
        def _():
            hl[:, side] = jnp.zeros_like(hl[:, side])

    def along_x(k, side, layer):
        step = 1 if side == 0 else -1
        return pltpu.make_async_remote_copy(
            src_ref=states[k].at[rows - 1 if side == 0 else 0, layer],
            dst_ref=hx.at[k, side, layer],
            send_sem=hx_s.at[k, side, layer], recv_sem=hx_r.at[k, side, layer],
            device_id=(lax.rem(t + step + tiles, tiles), d), device_id_type=MESH,
        )

    def along_l(k, side):
        step = 1 if side == 0 else -1
        return pltpu.make_async_remote_copy(
            src_ref=states[k].at[:, layers - 1 if side == 0 else 0],
            dst_ref=hl.at[k, side],
            send_sem=hl_s.at[k, side], recv_sem=hl_r.at[k, side],
            device_id=(t, lax.rem(d + step + depths, depths)), device_id_type=MESH,
        )

    send_x = (t < tiles - 1, t > 0)
    send_l = (d < depths - 1, d > 0)
    take_x = (t > 0, t < tiles - 1)
    take_l = (d > 0, d < depths - 1)

    def layer_start(k, layer):
        for side in range(2):
            pl.when(send_x[side])(along_x(k, side, layer).start)
        if layer == layers - 1:
            pl.when(send_l[0])(along_l(k, 0).start)
        if layer == 0:
            pl.when(send_l[1])(along_l(k, 1).start)

    def layer_wait(k, layer):
        if layer == 0:
            pl.when(take_l[0])(along_l(k, 0).wait_recv)
        if layer == layers - 1:
            pl.when(take_l[1])(along_l(k, 1).wait_recv)
        for side in range(2):
            pl.when(take_x[side])(along_x(k, side, layer).wait_recv)

    def halo_sent(k):
        for side in range(2):
            for layer in range(layers):
                pl.when(send_x[side])(along_x(k, side, layer).wait_send)
            pl.when(send_l[side])(along_l(k, side).wait_send)

    def top_copy(k, i):
        return pltpu.make_async_remote_copy(
            src_ref=top.at[k], dst_ref=top.at[k],
            send_sem=top_s.at[k, i], recv_sem=top_r.at[k],
            device_id=(t, i + 1), device_id_type=MESH,
        )

    def top_start(k):
        @pl.when(d == 0)
        def _():
            top[k] = states[k][:, 0]
            each(depths - 1, lambda i: top_copy(k, i).start())

    def top_wait(k):
        pl.when(d > 0)(lambda: top_copy(k, 0).wait_recv())

    def peer(i):
        return lax.rem(t + i + 1, tiles)

    def go_copy(part, other, to):
        return pltpu.make_async_remote_copy(
            src_ref=send.at[part, other], dst_ref=got.at[part, to],
            send_sem=go_s.at[part, other], recv_sem=go_r.at[part, to],
            device_id=(other, d), device_id_type=MESH,
        )

    def answer_copy(k, other, to):
        return pltpu.make_async_remote_copy(
            src_ref=ans.at[k, other], dst_ref=back.at[k, to],
            send_sem=an_s.at[k, other], recv_sem=an_r.at[k, to],
            device_id=(other, d), device_id_type=MESH,
        )

    def partial_copy(part, i):
        if part == 0:
            src, dst, ss, rs = scat.at[pl.ds(0, 8)], red_a, ra_s, ra_r
        else:
            src, dst, ss, rs = scat.at[pl.ds(8, 17)], red_b, rb_s, rb_r
        return pltpu.make_async_remote_copy(
            src_ref=src, dst_ref=dst.at[i], send_sem=ss, recv_sem=rs.at[i],
            device_id=(t, 0), device_id_type=MESH,
        )

    def reduce_wait(part):
        first, length = ((0, 8), (8, 17))[part]
        buffer = (red_a, red_b)[part]

        def add(i):
            partial_copy(part, i).wait_recv()
            scat[pl.ds(first, length)] += buffer[i]

        each(depths - 1, add)

    lane = iota((8, 8, 128), 2)
    sub = iota((8, 8, 128), 1)
    plus = iota((8, 8, 128), 0) % ORB < 2

    def stencil(k, l):
        layer_wait(k, l)
        field, out = states[k], states[k + 1]
        for x in range(rows):
            f = field[x, l]
            beside = field[x, l - 1] if l > 0 else hl[k, 0, x]
            beside += field[x, l + 1] if l < layers - 1 else hl[k, 1, x]
            beside += field[x - 1, l] if x > 0 else hx[k, 0, l]
            beside += field[x + 1, l] if x < rows - 1 else hx[k, 1, l]
            r = pltpu.roll(f, 1, 2)
            c = jnp.where(sub == 0, 0.0, pltpu.roll(r, 1, 1))
            beside += jnp.where(lane == 0, c, r)
            r = pltpu.roll(f, 127, 2)
            c = jnp.where(sub == 7, 0.0, pltpu.roll(r, 7, 1))
            beside += jnp.where(lane == 127, c, r)
            onsite = (disorder[x, l] - CHEMICAL)[None] * f - HOPPING * beside
            partner = jnp.concatenate([f[2:4], f[0:2], f[6:8], f[4:6]], axis=0)
            new = jnp.where(plus, onsite, -onsite) + PAIRING * partner
            if k > 0:
                new = 2.0 * new - states[k - 1][x, l]
            out[x, l] = new

    def hand_out(state, out):
        for x in range(rows):
            for l in range(layers):
                for q in range(8):
                    out[q % ORB, q // ORB, l, spread(x), :] = state[x, l, q]

    half_lane = iota((8, 128), 1) < 64

    def compact(part, values):
        pieces = jnp.concatenate(halves(values), axis=0)

        def one(g):
            chosen = [
                jnp.where(tile_of[...] == g * GROUP + i, pieces, 0.0).astype(jnp.bfloat16)
                for i in range(GROUP)
            ]
            found = product(jnp.concatenate(chosen, axis=0), rank_t[...], NT)
            for i in range(GROUP):
                at = i * 32
                mine = found[at : at + 16] + found[at + 16 : at + 32]
                if packed:
                    send[part, g * GROUP + i, 0:16] = mine[:, :128]
                    tail = pltpu.roll(mine[8:16, 128:], 64, 1)
                    send[part, g * GROUP + i, 16:24] = jnp.where(
                        half_lane, mine[0:8, 128:], tail
                    )
                else:
                    send[part, g * GROUP + i] = mine

        each(tiles // GROUP, one)

    def compact_start(part):
        each(tiles - 1, lambda i: go_copy(part, peer(i), t).start())
        got[part, t] = send[part, t]

    fetches[0].wait()
    owner = (iota((tiles, count), 0) == tile_of[...]).astype(jnp.float32)
    earlier = (iota((count, count), 0) < iota((count, count), 1)).astype(jnp.float32)
    before = product(owner.astype(jnp.bfloat16), earlier.astype(jnp.bfloat16))
    rank = jnp.sum(owner * before, axis=0, keepdims=True).astype(jnp.int32)
    rank_t[...] = (iota((slots, count), 0) == rank).astype(jnp.float32).astype(jnp.bfloat16)

    fetches[1].wait()
    for x in range(rows):
        for l in order_l:
            for q in range(8):
                s0[x, l, q] = sub_in[q % ORB, q // ORB, l, spread(x), :]
    pl.semaphore_wait(barrier, tiles - 1 + depths - 1)
    for l in order_l[: layers // 2]:
        layer_start(0, l)


    for fetch in fetches[2:5]:
        fetch.wait()
    for v in range(2):
        adatoms[:, v * count : (v + 1) * count] = ad_in[:, v, :]
    c = coupling[...]
    values = exact(c, adatoms[...])
    spot = spot_of[...].reshape(1, count)
    row = iota((8, count), 0)
    where = jnp.where(row == 0, (spot // 128 % 8 + 1).astype(jnp.float32), 0.0)
    where = jnp.where(row == 1, (spot // 1024 * 128 + spot % 128).astype(jnp.float32), where)
    compact(0, jnp.concatenate([values[:, :count], values[:, count:], where], axis=0))
    compact_start(0)
    for l in order_l[layers // 2 :]:
        layer_start(0, l)
    top_start(0)
    for fetch in fetches[5:]:
        fetch.wait()
    for x in range(rows):
        for l in range(layers):
            disorder[x, l] = dis_in[l, spread(x), :]

    wide = GROUP * each_wide

    def group(g):
        if tiles == GROUP:
            return slice(0, wide)
        return pl.ds(pl.multiple_of(g * wide, 128), wide)

    def arrived(part, g):
        blocks = [got[part, g * GROUP + i] for i in range(GROUP)]
        if packed:
            tails = []
            for i in range(0, GROUP, 2):
                one, two = blocks[i][16:24], blocks[i + 1][16:24]
                upper = jnp.where(half_lane, one, pltpu.roll(two, 64, 1))
                lower = jnp.where(half_lane, pltpu.roll(one, 64, 1), two)
                tails.append(jnp.concatenate([upper, lower], axis=0))
            blocks = [block_[0:16] for block_ in blocks] + tails
        return jnp.concatenate(blocks, axis=1)

    rows_b = [v * 8 + j * 4 + o for j in range(2) for v in range(2) for o in range(ORB)]

    def scatter(part, g):
        data = arrived(part, g)
        if part == 0:
            here = iota((8, wide), 0).astype(jnp.float32) + 1.0 == data[HIGH : HIGH + 1]
            high[:, group(g)] = here.astype(jnp.float32)
            low = iota((sites, wide), 0).astype(jnp.float32) == data[LOW : LOW + 1]
            low_t[:, group(g)] = low.astype(jnp.float32).astype(jnp.bfloat16)
        here = high[:, group(g)]
        start, terms = (0, 8) if part == 0 else (8, 17)
        first, second = halves(data)
        for at, q in enumerate(range(8) if part == 0 else rows_b):
            both = [here * piece[q : q + 1] for piece in (first, second)]
            lhs[at * 16 : at * 16 + 16] = jnp.concatenate(both, axis=0).astype(jnp.bfloat16)
        if part == 1:
            both = jnp.concatenate([here, jnp.zeros_like(here)], axis=0)
            lhs[256:272] = both.astype(jnp.bfloat16)
        total = product(lhs[: terms * 16], low_t[:, group(g)], NT)
        total = total.reshape(terms, 2, 8, sites)
        total = total[:, 0] + total[:, 1]
        for x in range(rows):
            mine = total[:, :, x * 128 : x * 128 + 128]
            if tiles == GROUP:
                scat[start : start + terms, x] = mine
            else:
                scat[start : start + terms, x] += mine

    if tiles > GROUP:
        scat[...] = jnp.zeros_like(scat)

    def scatter_all(part):
        each(tiles - 1, lambda i: go_copy(part, peer(i), peer(i)).wait_recv())
        each(tiles // GROUP, lambda g: scatter(part, g))
        pl.when(d > 0)(partial_copy(part, d - 1).start)

    def gather(k):
        top_wait(k)
        field = jnp.concatenate([top[k, x].reshape(64, 128) for x in range(rows)], axis=1)
        both = jnp.concatenate(halves(field), axis=0).astype(jnp.bfloat16)

        def one(g):
            found = product(both, low_t[:, group(g)])
            found = (found[:64] + found[64:]).reshape(8, 8, wide) * high[:, group(g)][None]
            found = jnp.sum(found, axis=1)
            for i in range(GROUP):
                if packed:
                    ans[k, g * GROUP + i, 0:8] = found[:, i * 128 : i * 128 + 128]
                    at = (GROUP + i // 2) * 128
                    tail = found[:, at : at + 128]
                    ans[k, g * GROUP + i, 8:16] = tail if i % 2 == 0 else pltpu.roll(tail, 64, 1)
                else:
                    ans[k, g * GROUP + i] = found[:, i * slots : (i + 1) * slots]

        each(tiles // GROUP, one)
        each(tiles - 1, lambda i: answer_copy(k, peer(i), t).start())
        back[k, t] = ans[k, t]

    def below(k):
        each(tiles - 1, lambda i: answer_copy(k, peer(i), peer(i)).wait_recv())
        if packed:
            mine = [back[k, :, i : i + 8].reshape(tiles * 8, 128) for i in (0, 8)]
            mine = jnp.concatenate(mine, axis=1)
        else:
            mine = back[k].reshape(tiles * 8, slots)
        first, second = halves(mine)
        both = jnp.concatenate([first, second], axis=0).astype(jnp.bfloat16)
        found = product(both, rank_t[...])
        found = (found[: tiles * 8] + found[tiles * 8 :]).reshape(tiles, 8, count)
        found = jnp.sum(found * owner.reshape(tiles, 1, count), axis=0)
        return jnp.concatenate([found[0:4], found[4:8]], axis=1)

    def adatom_part(k, vector):
        return exact(b, vector) + exact(ct, below(k))

    def hand_adatoms(vectors, out):
        for v in range(2):
            out[:, v, :] = vectors[:, v * count : (v + 1) * count]

    def mixed(pair, state, x):
        sums = []
        for v in range(2):
            for o in range(ORB):
                total = None
                for m in range(ORB):
                    term = pair[o : o + 1, m : m + 1] * state[x, 0, v * ORB + m]
                    total = term if total is None else total + term
                sums.append(total[None])
        return jnp.concatenate(sums, axis=0)

    b = block[...]
    cb = exact(c, b)
    proj[0:4] = cb
    proj[4:8] = exact(cb, b)
    pair1 = exact(c, c, NT)
    pair2 = exact(cb, c, NT)
    ct = exact((iota(b.shape, 0) == iota(b.shape, 1)).astype(jnp.float32), c, NT)
    values = exact(proj[...], adatoms[...])
    compact(1, jnp.concatenate([values[:, :count], values[:, count:]], axis=0))
    compact_start(1)

    scatter_all(0)
    def add_first():
        reduce_wait(0)
        for x in range(rows):
            s1[x, 0] += scat[0:8, x]

    def add_second():
        for x in range(rows):
            s2[x, 0] += scat[8:16, x]

    for l in order_l:
        stencil(0, l)
        if l == 0:
            pl.when(d == 0)(add_first)
            top_start(1)
        layer_start(1, l)

    scatter_all(1)
    gather(0)
    gather(1)

    @pl.when(d == 0)
    def _():
        reduce_wait(1)
        for x in range(rows):
            extra = scat[8:16, x] + scat[24, x][None] * mixed(pair1, s0, x)
            scat[8:16, x] = 2.0 * extra

    for l in order_l:
        stencil(1, l)
        if l == 0:
            pl.when(d == 0)(add_second)
            top_start(2)
        layer_start(2, l)

    hand_out(s2, sub_prev)
    a1[...] = adatom_part(0, adatoms[...])
    gather(2)

    @pl.when(d == 0)
    def _():
        for x in range(rows):
            pairs = mixed(pair2, s0, x) + mixed(pair1, s1, x)
            extra = scat[16:24, x] + scat[24, x][None] * pairs
            scat[16:24, x] = 2.0 * (2.0 * extra - scat[0:8, x])

    a2[...] = 2.0 * adatom_part(1, a1[...]) - adatoms[...]
    hand_adatoms(a2[...], ad_prev)
    for l in order_l:
        stencil(2, l)

    @pl.when(d == 0)
    def _():
        for x in range(rows):
            s3[x, 0] += scat[16:24, x]

    hand_out(s3, sub_last)

    hand_adatoms(2.0 * adatom_part(2, a2[...]) - a1[...], ad_last)

    for part in range(2):
        each(tiles - 1, lambda i: go_copy(part, peer(i), t).wait_send())
    for k in range(STEPS):
        halo_sent(k)
        each(tiles - 1, lambda i: answer_copy(k, peer(i), t).wait_send())

    @pl.when(d == 0)
    def _():
        for k in range(STEPS):
            each(depths - 1, lambda i: top_copy(k, i).wait_send())

    @pl.when(d > 0)
    def _():
        partial_copy(0, d - 1).wait_send()
        partial_copy(1, d - 1).wait_send()


def settle(*arrays):
    n = len(arrays)
    chunks = 2

    def body(*refs):
        held, sems = refs[2 * n : 3 * n], refs[3 * n]
        copies, leaves = [], []
        for i in range(n):
            step = refs[i].shape[0] // chunks
            for j in range(chunks):
                at = pl.ds(j * step, step)
                copies.append(
                    pltpu.make_async_copy(refs[i].at[at], held[i].at[at], sems.at[0, i, j])
                )
                leaves.append(
                    pltpu.make_async_copy(held[i].at[at], refs[n + i].at[at], sems.at[1, i, j])
                )
        for copy in copies:
            copy.start()
        for copy, leave in zip(copies, leaves):
            copy.wait()
            leave.start()
        for leave in leaves:
            leave.wait()

    anywhere = pl.BlockSpec(memory_space=pl.ANY)
    return pl.pallas_call(
        body,
        out_shape=tuple(jax.ShapeDtypeStruct(x.shape, x.dtype) for x in arrays),
        in_specs=[anywhere] * n,
        out_specs=(anywhere,) * n,
        scratch_shapes=[pltpu.VMEM(x.shape, x.dtype) for x in arrays]
        + [pltpu.SemaphoreType.DMA((2, n, chunks))],
        compiler_params=pltpu.CompilerParams(vmem_limit_bytes=56 << 20),
    )(*arrays)


def per_device(
    substrate_start, adatom_start, disorder, adatom_block, coupling, adatom_tile, adatom_spot
):
    tiles, depths = lax.axis_size("tile"), lax.axis_size("depth")
    count = adatom_spot.shape[0]
    orbs, vecs, layers, rows, cols = substrate_start.shape
    orba = adatom_block.shape[0]
    capacity = 2 * count // tiles
    slots = -(-capacity // 128) * 128
    f32 = jnp.float32

    def lined(x):
        lead = x.shape[:-2]
        n = len(lead)
        x = x.reshape(lead + (rows, 8, 128))
        x = x.transpose(tuple(range(n)) + (n + 1, n, n + 2))
        return x.reshape(lead + (8 * rows, 128))

    def unlined(x):
        lead = x.shape[:-2]
        n = len(lead)
        x = x.reshape(lead + (8, rows, 128))
        x = x.transpose(tuple(range(n)) + (n + 1, n, n + 2))
        return x.reshape(lead + (rows, cols))

    sites = lined(substrate_start)
    state = jax.ShapeDtypeStruct(sites.shape, f32)
    flat = jax.ShapeDtypeStruct(adatom_start.shape, f32)
    block_state = pltpu.VMEM((rows, layers, 8, 8, 128), f32)
    block_flat = pltpu.VMEM((orba, vecs * count), f32)
    packed = capacity == 192
    each_wide = capacity if packed else slots
    wide = GROUP * each_wide
    sent = (24, 128) if packed else (16, slots)
    answer = (16, 128) if packed else (8, slots)
    dma = pltpu.SemaphoreType.DMA
    vmem = pl.BlockSpec(memory_space=pltpu.VMEM)
    s2, s3, a2, a3 = pl.pallas_call(
        functools.partial(kernel, tiles, depths),
        out_shape=(state, state, flat, flat),
        in_specs=[pl.BlockSpec(memory_space=pltpu.HBM)] * 7,
        out_specs=(vmem,) * 4,
        scratch_shapes=[
            block_state, block_state, block_state, block_state,
            block_flat,
            pltpu.VMEM((rows, layers, 8, 128), f32),
            pltpu.VMEM((STEPS, 2, layers, 8, 8, 128), f32),
            pltpu.VMEM((STEPS, 2, rows, 8, 8, 128), f32),
            pltpu.VMEM((STEPS, rows, 8, 8, 128), f32),
            pltpu.VMEM((2, tiles) + sent, f32),
            pltpu.VMEM((2, tiles) + sent, f32),
            pltpu.VMEM((17 * 16, wide), jnp.bfloat16),
            pltpu.VMEM((rows * 128, tiles * each_wide), jnp.bfloat16),
            pltpu.VMEM((8, tiles * each_wide), f32),
            pltpu.VMEM((25, rows, 8, 128), f32),
            pltpu.VMEM((depths - 1, 8, rows, 8, 128), f32),
            pltpu.VMEM((depths - 1, 17, rows, 8, 128), f32),
            pltpu.VMEM((STEPS, tiles) + answer, f32),
            pltpu.VMEM((STEPS, tiles) + answer, f32),
            pltpu.VMEM((8, orba), f32),
            pltpu.VMEM((slots, count), jnp.bfloat16),
            block_flat, block_flat,
            pltpu.VMEM(sites.shape, f32),
            pltpu.VMEM(adatom_start.shape, f32),
            pltpu.VMEM((layers, 8 * rows, 128), f32),
            pltpu.VMEM(adatom_block.shape, f32),
            pltpu.VMEM(coupling.shape, f32),
            pltpu.VMEM((1, count), jnp.int32),
            pltpu.VMEM((count,), jnp.int32),
            dma((7,)),
            dma((STEPS, 2, layers)), dma((STEPS, 2, layers)), dma((STEPS, 2)), dma((STEPS, 2)),
            dma((STEPS, depths - 1)), dma((STEPS,)),
            dma((2, tiles)), dma((2, tiles)),
            dma, dma((depths - 1,)), dma, dma((depths - 1,)),
            dma((STEPS, tiles)), dma((STEPS, tiles)),
        ],
        compiler_params=pltpu.CompilerParams(
            collective_id=0, has_side_effects=True, vmem_limit_bytes=56 << 20
        ),
    )(
        sites, adatom_start, lined(disorder), adatom_block, coupling,
        adatom_tile.reshape(1, count), adatom_spot,
    )
    s2, s3, a2, a3 = settle(s2, s3, a2, a3)
    return unlined(s2), unlined(s3), a2, a3


def solution(mesh):
    in_specs = (
        P(None, None, "depth", "tile", None),
        P(None, None, ("tile", "depth")),
        P("depth", "tile", None),
        P(),
        P(),
        P(("tile", "depth"), None),
        P(("tile", "depth")),
    )
    out_specs = (
        P(None, None, "depth", "tile", None),
        P(None, None, "depth", "tile", None),
        P(None, None, ("tile", "depth")),
        P(None, None, ("tile", "depth")),
    )
    return jax.shard_map(
        per_device, mesh=mesh, in_specs=in_specs, out_specs=out_specs, check_vma=False
    )
```
